512 devices in a mesh: blk: 64 (over x, z_hi, y), head: 8 (over z_lo, core).
Axes of the slice: x: 4, y: 8, z: 8 (z_hi: 2, z_lo: 4; z = z_hi * 4 + z_lo), core: 2. Of those that a mesh axis runs over, the one named last changes fastest.
Arguments:
- queries: bfloat16 [65536, 2048], P(('blk', 'head')), may hold values from -4.7 to 4.7
- keys: bfloat16 [65536, 2048], P(('blk', 'head')), may hold values from -4.7 to 4.7
- values: bfloat16 [65536, 2048], P(('blk', 'head')), may hold values from -5 to 5
- w_out: bfloat16 [2048, 1600], P('head', 'blk'), may hold values from -1.5 to 1.5
Outputs:
- projected: bfloat16 [65536, 1600], P(('blk', 'head'))
The draws below stay inside these ranges and needn't reach their ends.
All inputs are finite; a program needn't handle non-finite values.
Results may differ from the reference program's by a relative error of at most 0.0075.
Values may be sent and summed in bfloat16 or wider, within the bound.
No kernel may reach another device: no remote copies, remote signals or barrier semaphores. Data moves between devices by JAX's collectives and lax.ppermute only.
A program may use at most 64 MiB of HBM per device.

```python
import jax
import jax.numpy as jnp
from jax import lax

HEADS = 16
HDIM = 128
DWIN = 1600
TOK_DEV = 128
HD = 2048
TOKENS = 65536
N_BLK = 64
N_HEAD = 8


def draw_queries(key, part):
    key = jax.random.fold_in(key, 1)
    sample_field = 1.3 * jax.random.truncated_normal(key, -3.4, 3.4, (TOKENS, HD), jnp.float32)
    return sample_field.astype(jnp.bfloat16)


def draw_keys(key, part):
    key = jax.random.fold_in(key, 2)
    sample_field = 1.3 * jax.random.truncated_normal(key, -3.4, 3.4, (TOKENS, HD), jnp.float32)
    return sample_field.astype(jnp.bfloat16)


def levels(stream_key, extent, shards, low, high):
    def one(position, parts):
        steps = jax.random.uniform(jax.random.fold_in(jax.random.fold_in(stream_key, 6), position), (parts,), jnp.float32, low / len(shards), high / len(shards))
        return jnp.repeat(jnp.exp(steps), extent[position] // parts).reshape((-1,) + (1,) * (len(extent) - position - 1))

    gain = one(*shards[0])
    for cut in shards[1:]:
        gain = gain * one(*cut)
    return gain


def gaussian(rng, extent, scale, limit, shards=(), kind=jnp.bfloat16):
    drawn = scale * jax.random.normal(rng, extent, jnp.float32)
    if shards:
        drawn = drawn * levels(rng, extent, shards, -0.22, 0.18)
    return jnp.clip(drawn, -limit, limit).astype(kind)


def setup_inputs(seed: int = 0) -> dict:
    key_list = jax.random.split(jax.random.key(seed), 5)
    queries = draw_queries(jax.random.fold_in(key_list[4], 71), 0)
    keys = draw_keys(jax.random.fold_in(key_list[4], 71), 0)
    values = gaussian(key_list[2], (TOKENS, HD), 1.0, 5.0, ((0, 512),))
    w_out = gaussian(key_list[3], (HD, DWIN), 0.25, 1.5, ((0, 8), (1, 64)))
    return {"queries": queries, "keys": keys, "values": values, "w_out": w_out}


def attend_rows(query_rows, near_keys, near_values, key_ok):
    scores = jnp.einsum("qhd,khd->hqk", query_rows.astype(jnp.float32), near_keys.astype(jnp.float32)) * (HDIM ** -0.5)
    scores = jnp.where(key_ok[None, None, :], scores, -1e30)
    largest = jnp.max(scores, axis=2, keepdims=True)
    raised = jnp.exp(scores - largest)
    totals = jnp.sum(raised, axis=2)
    probs = raised.astype(jnp.bfloat16).astype(jnp.float32)
    weighted = jnp.einsum("hqk,khd->qhd", probs, near_values.astype(jnp.float32))
    return (weighted / jnp.transpose(totals)[:, :, None]).astype(jnp.bfloat16)


def reference(queries, keys, values, w_out):
    count = N_BLK
    block_len = TOK_DEV * N_HEAD
    width = HEADS * HDIM
    q_blocks = queries.reshape(count, block_len, HEADS, HDIM)
    zero_block = jnp.zeros((1, block_len, width), jnp.bfloat16)
    padded_keys = jnp.concatenate([zero_block, keys.reshape(count, block_len, width), zero_block], 0)
    padded_values = jnp.concatenate([zero_block, values.reshape(count, block_len, width), zero_block], 0)
    group_width = width // N_HEAD
    w_groups = w_out.reshape(N_HEAD, group_width, DWIN).astype(jnp.float32)

    def one_block(index):
        query_rows = lax.dynamic_index_in_dim(q_blocks, index, 0, keepdims=False)
        near_keys = lax.dynamic_slice_in_dim(padded_keys, index, 3, 0).reshape(3 * block_len, HEADS, HDIM)
        near_values = lax.dynamic_slice_in_dim(padded_values, index, 3, 0).reshape(3 * block_len, HEADS, HDIM)
        owner = index - 1 + jnp.arange(3 * block_len, dtype=jnp.int32) // block_len
        key_ok = (owner >= 0) & (owner < count)
        context = attend_rows(query_rows, near_keys, near_values, key_ok)
        split_context = context.reshape(block_len, N_HEAD, group_width).astype(jnp.float32)
        partials = jnp.einsum("tgw,gwc->gtc", split_context, w_groups)
        partials = lax.optimization_barrier(partials.astype(jnp.bfloat16)).astype(jnp.float32)
        return jnp.sum(partials, axis=0).astype(jnp.bfloat16)

    result = lax.map(one_block, jnp.arange(count, dtype=jnp.int32))
    return result.reshape(count * block_len, DWIN)
```

```python
import functools
import math

import jax
import jax.numpy as jnp
from jax import lax
from jax.experimental import pallas as pl
from jax.experimental.pallas import tpu as pltpu
from jax.sharding import Mesh, PartitionSpec as P

HDIM = 128
LOG2E = 1.4426950408889634
FACTOR = LOG2E / math.sqrt(HDIM)
AXES = ("x", "zh", "y", "zl", "c")
SIZES = (4, 2, 8, 4, 2)
BLK = ("x", "zh", "y")
HEAD = ("zl", "c")
TILE = 256
DIMS_NT = (((1,), (1,)), ((), ()))
DIMS_TN = (((0,), (0,)), ((), ()))
VMEM = 48 * 1024 * 1024


def own_kernel(q_ref, k_ref, v_ref, acc_ref, m_ref, l_ref):
    scores = lax.dot_general(k_ref[...], q_ref[...], DIMS_NT, preferred_element_type=jnp.float32)
    largest = jnp.max(scores, axis=0, keepdims=True) * FACTOR
    raised = jnp.exp2(scores * FACTOR - largest)
    m_ref[0] = jnp.broadcast_to(largest, m_ref.shape[1:])
    l_ref[0] = jnp.broadcast_to(jnp.sum(raised, axis=0, keepdims=True), l_ref.shape[1:])
    acc_ref[0] = lax.dot_general(
        v_ref[...], raised.astype(jnp.bfloat16), DIMS_TN, preferred_element_type=jnp.float32
    )


def own_attention(q, k, v):
    rows, width = q.shape
    heads = width // HDIM
    return pl.pallas_call(
        own_kernel,
        grid=(heads, rows // TILE),
        in_specs=[
            pl.BlockSpec((TILE, HDIM), lambda h, i: (i, h)),
            pl.BlockSpec((rows, HDIM), lambda h, i: (0, h)),
            pl.BlockSpec((rows, HDIM), lambda h, i: (0, h)),
        ],
        out_specs=[
            pl.BlockSpec((1, HDIM, TILE), lambda h, i: (h, 0, i)),
            pl.BlockSpec((1, 8, TILE), lambda h, i: (h, 0, i)),
            pl.BlockSpec((1, 8, TILE), lambda h, i: (h, 0, i)),
        ],
        out_shape=[
            jax.ShapeDtypeStruct((heads, HDIM, rows), jnp.float32),
            jax.ShapeDtypeStruct((heads, 8, rows), jnp.float32),
            jax.ShapeDtypeStruct((heads, 8, rows), jnp.float32),
        ],
        compiler_params=pltpu.CompilerParams(vmem_limit_bytes=VMEM),
        cost_estimate=pl.CostEstimate(
            flops=4 * rows * rows * width, bytes_accessed=6 * rows * width, transcendentals=rows * rows * heads
        ),
        name="own_attention",
    )(q, k, v)


def near_kernel(ok_ref, q_ref, kp_ref, vp_ref, kn_ref, vn_ref, acc_ref, m_ref, l_ref, out_ref):
    far = jnp.float32(1e30)
    q = q_ref[...]
    m = m_ref[0][:1]
    sides = ((kp_ref, vp_ref, ok_ref[0] > 0), (kn_ref, vn_ref, ok_ref[1] > 0))
    scores = []
    for k_ref, _, ok in sides:
        s = lax.dot_general(k_ref[...], q, DIMS_NT, preferred_element_type=jnp.float32)
        scores.append(s)
        m = jnp.maximum(m, jnp.where(ok, jnp.max(s, axis=0, keepdims=True) * FACTOR, -far))
    alpha = jnp.exp2(m_ref[0][:1] - m)
    total = l_ref[0][:1] * alpha
    acc = acc_ref[0] * alpha
    for s, (_, v_ref, ok) in zip(scores, sides):
        raised = jnp.exp2(s * FACTOR - jnp.where(ok, m, far))
        total += jnp.sum(raised, axis=0, keepdims=True)
        acc += lax.dot_general(
            v_ref[...], raised.astype(jnp.bfloat16), DIMS_TN, preferred_element_type=jnp.float32
        )
    result = (acc / total).astype(jnp.bfloat16)
    tok = out_ref.shape[2]
    for part in range(out_ref.shape[0]):
        out_ref[part] = result[:, part * tok : (part + 1) * tok]


def near_attention(ok, q, kp, vp, kn, vn, acc, m, l, tok):
    rows, width = q.shape
    heads = width // HDIM
    side = pl.BlockSpec((rows, HDIM), lambda h, i: (0, h))
    row = pl.BlockSpec((1, 8, TILE), lambda h, i: (h, 0, i))
    return pl.pallas_call(
        near_kernel,
        grid=(heads, rows // TILE),
        in_specs=[
            pl.BlockSpec(memory_space=pltpu.SMEM),
            pl.BlockSpec((TILE, HDIM), lambda h, i: (i, h)),
            side,
            side,
            side,
            side,
            pl.BlockSpec((1, HDIM, TILE), lambda h, i: (h, 0, i)),
            row,
            row,
        ],
        out_specs=pl.BlockSpec((TILE // tok, HDIM, tok), lambda h, i: (i, h, 0)),
        out_shape=jax.ShapeDtypeStruct((rows // tok, width, tok), jnp.bfloat16),
        compiler_params=pltpu.CompilerParams(vmem_limit_bytes=VMEM),
        cost_estimate=pl.CostEstimate(
            flops=8 * rows * rows * width, bytes_accessed=14 * rows * width, transcendentals=2 * rows * rows * heads
        ),
        name="near_attention",
    )(ok, q, kp, vp, kn, vn, acc, m, l)


def project_kernel(w_ref, ctx_ref, out_ref):
    total = None
    for c in range(w_ref.shape[1]):
        part = jnp.dot(w_ref[0, c], ctx_ref[c], preferred_element_type=jnp.float32)
        total = part if total is None else total + part
    out_ref[...] = total.astype(jnp.bfloat16)


def project(w, ctx):
    parts, cores, rows, depth = w.shape
    tok = ctx.shape[2]
    return pl.pallas_call(
        project_kernel,
        grid=(parts,),
        in_specs=[
            pl.BlockSpec((1, cores, rows, depth), lambda i: (i, 0, 0, 0)),
            pl.BlockSpec((cores, depth, tok), lambda i: (0, 0, 0)),
        ],
        out_specs=pl.BlockSpec((rows, tok), lambda i: (i, 0)),
        out_shape=jax.ShapeDtypeStruct((parts * rows, tok), jnp.bfloat16),
        compiler_params=pltpu.CompilerParams(vmem_limit_bytes=VMEM),
        cost_estimate=pl.CostEstimate(
            flops=2 * parts * rows * depth * cores * tok, bytes_accessed=2 * parts * rows * depth * cores, transcendentals=0
        ),
        name="project",
    )(w, ctx)


def head_split(value):
    tok = value.shape[0]
    chunks = value.reshape(tok, 8, -1).transpose(1, 0, 2)
    moved = lax.all_to_all(chunks, HEAD, split_axis=0, concat_axis=0)
    return moved.reshape(8 * tok, -1)


def gather_w(w):
    wt = w.T
    cols, depth = wt.shape
    a = lax.all_gather(wt, ("zh", "zl"))
    a = a.reshape(2, 4, cols, depth).transpose(0, 2, 1, 3).reshape(2 * cols, 4 * depth)
    b = lax.all_gather(a, "y")
    b = b.reshape(8, 2, cols, 4 * depth).transpose(1, 0, 2, 3).reshape(16 * cols, 4 * depth)
    return lax.all_gather(b, ("x", "c")).reshape(4, 2, 16 * cols, 4 * depth)


def local(queries, keys, values, w_out):
    tok = queries.shape[0]
    weight = gather_w(w_out)
    k = head_split(keys)
    v = head_split(values)
    q = head_split(queries)
    n_blk = 64
    up = [(i, i + 1) for i in range(n_blk - 1)]
    down = [(i + 1, i) for i in range(n_blk - 1)]
    kp, kn = lax.ppermute(k, BLK, up), lax.ppermute(k, BLK, down)
    vp, vn = lax.ppermute(v, BLK, up), lax.ppermute(v, BLK, down)
    here = lax.axis_index(BLK)
    ok = jnp.stack([here > 0, here < n_blk - 1]).astype(jnp.int32)
    acc, m, l = own_attention(q, k, v)
    ctx = near_attention(ok, q, kp, vp, kn, vn, acc, m, l, tok)
    moved = lax.all_to_all(ctx, HEAD, split_axis=0, concat_axis=0)
    width = moved.shape[1]
    by_core = moved.reshape(4, 2, width, tok).transpose(1, 0, 2, 3).reshape(2, 4 * width, tok)
    return project(weight, by_core).T


def solution(mesh):
    cut = Mesh(mesh.devices.reshape(SIZES), AXES)
    return jax.shard_map(
        local,
        mesh=cut,
        in_specs=(P(AXES, None), P(AXES, None), P(AXES, None), P(HEAD, BLK)),
        out_specs=P(AXES, None),
        check_vma=False,
    )
```

```python
import functools
import math

import jax
import jax.numpy as jnp
from jax import lax
from jax.experimental import pallas as pl
from jax.experimental.pallas import tpu as pltpu
from jax.sharding import Mesh, PartitionSpec as P

HDIM = 128
LOG2E = 1.4426950408889634
FACTOR = LOG2E / math.sqrt(HDIM)
AXES = ("x", "zh", "y", "zl", "c")
SIZES = (4, 2, 8, 4, 2)
BLK = ("x", "zh", "y")
HEAD = ("zl", "c")
TILE = 256
DIMS_NT = (((1,), (1,)), ((), ()))
DIMS_TN = (((0,), (0,)), ((), ()))
VMEM = 32 * 1024 * 1024
EXTRA = 16


def own_kernel(q_ref, k_ref, v_ref, acc_ref, m_ref, l_ref):
    scores = lax.dot_general(k_ref[...], q_ref[...], DIMS_NT, preferred_element_type=jnp.float32)
    largest = jnp.max(scores, axis=0, keepdims=True) * FACTOR
    raised = jnp.exp2(scores * FACTOR - largest)
    m_ref[0] = jnp.broadcast_to(largest, m_ref.shape[1:])
    l_ref[0] = jnp.broadcast_to(jnp.sum(raised, axis=0, keepdims=True), l_ref.shape[1:])
    acc_ref[0] = lax.dot_general(
        v_ref[...], raised.astype(jnp.bfloat16), DIMS_TN, preferred_element_type=jnp.float32
    )


def own_attention(q, k, v):
    rows, width = q.shape
    heads = width // HDIM
    return pl.pallas_call(
        own_kernel,
        grid=(heads, rows // TILE),
        in_specs=[
            pl.BlockSpec((TILE, HDIM), lambda h, i: (i, h)),
            pl.BlockSpec((rows, HDIM), lambda h, i: (0, h)),
            pl.BlockSpec((rows, HDIM), lambda h, i: (0, h)),
        ],
        out_specs=[
            pl.BlockSpec((1, HDIM, TILE), lambda h, i: (h, 0, i)),
            pl.BlockSpec((1, 8, TILE), lambda h, i: (h, 0, i)),
            pl.BlockSpec((1, 8, TILE), lambda h, i: (h, 0, i)),
        ],
        out_shape=[
            jax.ShapeDtypeStruct((heads, HDIM, rows), jnp.float32),
            jax.ShapeDtypeStruct((heads, 8, rows), jnp.float32),
            jax.ShapeDtypeStruct((heads, 8, rows), jnp.float32),
        ],
        compiler_params=pltpu.CompilerParams(vmem_limit_bytes=VMEM),
        cost_estimate=pl.CostEstimate(
            flops=rows * width, bytes_accessed=rows * width, transcendentals=0
        ),
        name="own_attention",
    )(q, k, v)


def near_kernel(ok_ref, q_ref, kp_ref, vp_ref, kn_ref, vn_ref, acc_ref, m_ref, l_ref, out_ref):
    far = jnp.float32(1e30)
    q = q_ref[...]
    m = m_ref[0][:1]
    sides = ((kp_ref, vp_ref, ok_ref[0] > 0), (kn_ref, vn_ref, ok_ref[1] > 0))
    scores = []
    for k_ref, _, ok in sides:
        s = lax.dot_general(k_ref[...], q, DIMS_NT, preferred_element_type=jnp.float32)
        scores.append(s)
        m = jnp.maximum(m, jnp.where(ok, jnp.max(s, axis=0, keepdims=True) * FACTOR, -far))
    alpha = jnp.exp2(m_ref[0][:1] - m)
    total = l_ref[0][:1] * alpha
    acc = acc_ref[0] * alpha
    for s, (_, v_ref, ok) in zip(scores, sides):
        raised = jnp.exp2(s * FACTOR - jnp.where(ok, m, far))
        total += jnp.sum(raised, axis=0, keepdims=True)
        acc += lax.dot_general(
            v_ref[...], raised.astype(jnp.bfloat16), DIMS_TN, preferred_element_type=jnp.float32
        )
    result = (acc / total).astype(jnp.bfloat16)
    tok = out_ref.shape[2]
    for part in range(out_ref.shape[0]):
        out_ref[part] = result[:, part * tok : (part + 1) * tok]


def near_attention(ok, q, kp, vp, kn, vn, acc, m, l, tok):
    rows, width = q.shape
    heads = width // HDIM
    side = pl.BlockSpec((rows, HDIM), lambda h, i: (0, h))
    row = pl.BlockSpec((1, 8, TILE), lambda h, i: (h, 0, i))
    return pl.pallas_call(
        near_kernel,
        grid=(heads, rows // TILE),
        in_specs=[
            pl.BlockSpec(memory_space=pltpu.SMEM),
            pl.BlockSpec((TILE, HDIM), lambda h, i: (i, h)),
            side,
            side,
            side,
            side,
            pl.BlockSpec((1, HDIM, TILE), lambda h, i: (h, 0, i)),
            row,
            row,
        ],
        out_specs=pl.BlockSpec((TILE // tok, HDIM, tok), lambda h, i: (i, h, 0)),
        out_shape=jax.ShapeDtypeStruct((rows // tok, width, tok), jnp.bfloat16),
        compiler_params=pltpu.CompilerParams(vmem_limit_bytes=VMEM),
        cost_estimate=pl.CostEstimate(
            flops=8 * rows * rows * width, bytes_accessed=14 * rows * width, transcendentals=2 * rows * rows * heads
        ),
        name="near_attention",
    )(ok, q, kp, vp, kn, vn, acc, m, l)


def project_kernel(w_ref, ctx_ref, out_ref):
    total = None
    groups, width, tok = ctx_ref.shape
    half = width // w_ref.shape[1]
    for h in range(w_ref.shape[1]):
        ctx = ctx_ref[:, h * half : (h + 1) * half, :].reshape(groups * half, tok)
        part = jnp.dot(w_ref[0, h], ctx, preferred_element_type=jnp.float32)
        total = part if total is None else total + part
    out_ref[...] = total.astype(jnp.bfloat16)


def project(w, ctx):
    parts, cores, rows, depth = w.shape
    tok = ctx.shape[2]
    return pl.pallas_call(
        project_kernel,
        grid=(parts,),
        in_specs=[
            pl.BlockSpec((1, cores, rows, depth), lambda i: (i, 0, 0, 0)),
            pl.BlockSpec(ctx.shape, lambda i: (0, 0, 0)),
        ],
        out_specs=pl.BlockSpec((rows, tok), lambda i: (i, 0)),
        out_shape=jax.ShapeDtypeStruct((parts * rows, tok), jnp.bfloat16),
        compiler_params=pltpu.CompilerParams(vmem_limit_bytes=VMEM),
        cost_estimate=pl.CostEstimate(
            flops=2 * parts * rows * depth * cores * tok, bytes_accessed=2 * parts * rows * depth * cores, transcendentals=0
        ),
        name="project",
    )(w, ctx)


def pack_kernel(k_ref, w_ref, out_ref):
    groups, rows, width = out_ref.shape
    tok = k_ref.shape[0]
    half = width // 2
    cols = w_ref.shape[0]
    low = rows - tok
    for g in range(groups):
        out_ref[g, :tok, :] = k_ref[:, g * width : (g + 1) * width]
        part = w_ref[:, (g % 2) * half : (g % 2 + 1) * half]
        out_ref[g, tok:, :half] = part[:low]
        out_ref[g, tok : tok + cols - low, half:] = part[low:]
        out_ref[g, tok + cols - low :, half:] = jnp.zeros((2 * low - cols, half), out_ref.dtype)


def pack(k, wt):
    tok, width = k.shape[0], wt.shape[1]
    return pl.pallas_call(
        pack_kernel,
        out_shape=jax.ShapeDtypeStruct((8, tok + EXTRA, width), k.dtype),
        compiler_params=pltpu.CompilerParams(vmem_limit_bytes=VMEM),
        name="pack",
    )(k, wt)


def unpack_kernel(in_ref, k_ref, w_ref):
    groups, rows, width = in_ref.shape
    tok = k_ref.shape[1]
    low = rows - tok
    half = width // 2
    for g in range(groups):
        k_ref[g] = in_ref[g, :tok, :]
        w_ref[:low, g * half : (g + 1) * half] = in_ref[g, tok:, :half]
        w_ref[low:, g * half : (g + 1) * half] = in_ref[g, tok:, half:]


def unpack(moved):
    groups, rows, width = moved.shape
    tok = rows - EXTRA
    return pl.pallas_call(
        unpack_kernel,
        out_shape=[
            jax.ShapeDtypeStruct((groups, tok, width), moved.dtype),
            jax.ShapeDtypeStruct((2 * EXTRA, groups * width // 2), moved.dtype),
        ],
        compiler_params=pltpu.CompilerParams(vmem_limit_bytes=VMEM),
        name="unpack",
    )(moved)


def to_heads(chunks):
    return lax.all_to_all(chunks, HEAD, split_axis=0, concat_axis=0)


def split_heads(value):
    tok = value.shape[0]
    return value.reshape(tok, 8, -1).transpose(1, 0, 2)


def local(queries, keys, values, w_out):
    tok = queries.shape[0]
    cols, depth = w_out.shape[1], 4 * w_out.shape[0]
    n_blk = 64
    up = [(i, i + 1) for i in range(n_blk - 1)]
    down = [(i + 1, i) for i in range(n_blk - 1)]
    here = lax.axis_index(BLK)
    ok = jnp.stack([here > 0, here < n_blk - 1]).astype(jnp.int32)
    k, w_rows = unpack(to_heads(pack(keys, w_out.T)))
    k = k.reshape(8 * tok, -1)

    other = lax.ppermute(w_rows, "zh", [(0, 1), (1, 0)])
    kp, kn = lax.ppermute(k, BLK, up), lax.ppermute(k, BLK, down)
    values, k = lax.optimization_barrier((values, k))
    v = to_heads(split_heads(values)).reshape(8 * tok, -1)
    first = lax.axis_index("zh") == 0
    pair = jnp.stack([jnp.where(first, w_rows, other), jnp.where(first, other, w_rows)])
    line = lax.all_gather(pair.reshape(-1, depth), "y").reshape(8, 2, -1, depth)
    kp, kn, v, queries = lax.optimization_barrier((kp, kn, v, queries))

    vp, vn = lax.ppermute(v, BLK, up), lax.ppermute(v, BLK, down)
    q = to_heads(split_heads(queries)).reshape(8 * tok, -1)
    acc, m, l = own_attention(q, k, v)
    line, acc, vp, vn = lax.optimization_barrier((line, acc, vp, vn))
    line = line[:, :, :cols].transpose(1, 0, 2, 3).reshape(16 * cols, depth)
    line, acc = lax.optimization_barrier((line, acc))
    weight = lax.all_gather(line, ("x", "c")).reshape(4, 2, 16 * cols, depth)
    ctx = near_attention(ok, q, kp, vp, kn, vn, acc, m, l, tok)
    return project(weight, to_heads(ctx)).T


def solution(mesh):
    cut = Mesh(mesh.devices.reshape(SIZES), AXES)
    return jax.shard_map(
        local,
        mesh=cut,
        in_specs=(P(AXES, None), P(AXES, None), P(AXES, None), P(HEAD, BLK)),
        out_specs=P(AXES, None),
        check_vma=False,
    )
```

```python
import functools
import math

import jax
import jax.numpy as jnp
from jax import lax
from jax.experimental import pallas as pl
from jax.experimental.pallas import tpu as pltpu
from jax.sharding import Mesh, PartitionSpec as P

HDIM = 128
LOG2E = 1.4426950408889634
FACTOR = LOG2E / math.sqrt(HDIM)
AXES = ("x", "zh", "y", "zl", "c")
SIZES = (4, 2, 8, 4, 2)
BLK = ("x", "zh", "y")
HEAD = ("zl", "c")
TILE = 256
DIMS_NT = (((1,), (1,)), ((), ()))
DIMS_TN = (((0,), (0,)), ((), ()))
VMEM = 32 * 1024 * 1024
N_BLK = 64


def attend(parts, q, carry):
    far = jnp.float32(1e30)
    scores, m = [], None if carry is None else carry[1]
    for k, _, ok in parts:
        s = lax.dot_general(k, q, DIMS_NT, preferred_element_type=jnp.float32)
        scores.append(s)
        largest = jnp.max(s, axis=0, keepdims=True) * FACTOR
        if ok is not None:
            largest = jnp.where(ok, largest, -far)
        m = largest if m is None else jnp.maximum(m, largest)
    acc = total = None
    if carry is not None:
        alpha = jnp.exp2(carry[1] - m)
        acc, total = carry[0] * alpha, carry[2] * alpha
    for s, (_, v, ok) in zip(scores, parts):
        raised = jnp.exp2(s * FACTOR - (m if ok is None else jnp.where(ok, m, far)))
        part = lax.dot_general(v, raised.astype(jnp.bfloat16), DIMS_TN, preferred_element_type=jnp.float32)
        summed = jnp.sum(raised, axis=0, keepdims=True)
        acc, total = (part, summed) if acc is None else (acc + part, total + summed)
    return acc, m, total


def pair_kernel(ok_ref, q_ref, k_ref, v_ref, acc_ref, m_ref, l_ref):
    chunks, tok = k_ref.shape[0] // 2, k_ref.shape[1]
    parts = []
    for p in range(2):
        span = slice(p * chunks, (p + 1) * chunks)
        parts.append(
            (k_ref[span].reshape(chunks * tok, HDIM), v_ref[span].reshape(chunks * tok, HDIM), ok_ref[p] > 0)
        )
    acc, m, total = attend(parts, q_ref[...], None)
    acc_ref[0] = acc
    m_ref[0] = jnp.broadcast_to(m, m_ref.shape[1:])
    l_ref[0] = jnp.broadcast_to(total, l_ref.shape[1:])


def sides(kv):
    block = (kv.shape[0], kv.shape[1] // 2, HDIM)
    return [pl.BlockSpec(block, lambda h, i: (0, 0, h)), pl.BlockSpec(block, lambda h, i: (0, 1, h))]


def pair_attention(ok, q, kv):
    rows, width = q.shape
    heads = width // HDIM
    row = pl.BlockSpec((1, 8, TILE), lambda h, i: (h, 0, i))
    return pl.pallas_call(
        pair_kernel,
        grid=(heads, rows // TILE),
        in_specs=[
            pl.BlockSpec(memory_space=pltpu.SMEM),
            pl.BlockSpec((TILE, HDIM), lambda h, i: (i, h)),
            *sides(kv),
        ],
        out_specs=[pl.BlockSpec((1, HDIM, TILE), lambda h, i: (h, 0, i)), row, row],
        out_shape=[
            jax.ShapeDtypeStruct((heads, HDIM, rows), jnp.float32),
            jax.ShapeDtypeStruct((heads, 8, rows), jnp.float32),
            jax.ShapeDtypeStruct((heads, 8, rows), jnp.float32),
        ],
        compiler_params=pltpu.CompilerParams(vmem_limit_bytes=VMEM),
        cost_estimate=pl.CostEstimate(flops=rows * width, bytes_accessed=rows * width, transcendentals=0),
        name="pair_attention",
    )(ok, q, kv, kv)


def last_kernel(q_ref, k_ref, v_ref, acc_ref, m_ref, l_ref, out_ref):
    carry = (acc_ref[0], m_ref[0][:1], l_ref[0][:1])
    rows = k_ref.shape[0] * k_ref.shape[1]
    part = (k_ref[...].reshape(rows, HDIM), v_ref[...].reshape(rows, HDIM), None)
    acc, _, total = attend([part], q_ref[...], carry)
    result = (acc / total).astype(jnp.bfloat16)
    tok = out_ref.shape[2]
    for part in range(out_ref.shape[0]):
        out_ref[part] = result[:, part * tok : (part + 1) * tok]


def last_attention(q, kv, acc, m, l, tok):
    rows, width = q.shape
    heads = width // HDIM
    row = pl.BlockSpec((1, 8, TILE), lambda h, i: (h, 0, i))
    return pl.pallas_call(
        last_kernel,
        grid=(heads, rows // TILE),
        in_specs=[
            pl.BlockSpec((TILE, HDIM), lambda h, i: (i, h)),
            *sides(kv),
            pl.BlockSpec((1, HDIM, TILE), lambda h, i: (h, 0, i)),
            row,
            row,
        ],
        out_specs=pl.BlockSpec((TILE // tok, HDIM, tok), lambda h, i: (i, h, 0)),
        out_shape=jax.ShapeDtypeStruct((rows // tok, width, tok), jnp.bfloat16),
        compiler_params=pltpu.CompilerParams(vmem_limit_bytes=VMEM),
        cost_estimate=pl.CostEstimate(
            flops=4 * rows * rows * width, bytes_accessed=14 * rows * width, transcendentals=rows * rows * heads
        ),
        name="last_attention",
    )(q, kv, kv, acc, m, l)


def project_kernel(w_ref, ctx_ref, out_ref):
    total = None
    groups, width, tok = ctx_ref.shape
    half = width // w_ref.shape[1]
    for h in range(w_ref.shape[1]):
        ctx = ctx_ref[:, h * half : (h + 1) * half, :].reshape(groups * half, tok)
        part = jnp.dot(w_ref[0, h], ctx, preferred_element_type=jnp.float32)
        total = part if total is None else total + part
    out_ref[...] = total.astype(jnp.bfloat16)


def project(w, ctx):
    parts, cores, rows, depth = w.shape
    tok = ctx.shape[2]
    return pl.pallas_call(
        project_kernel,
        grid=(parts,),
        in_specs=[
            pl.BlockSpec((1, cores, rows, depth), lambda i: (i, 0, 0, 0)),
            pl.BlockSpec(ctx.shape, lambda i: (0, 0, 0)),
        ],
        out_specs=pl.BlockSpec((rows, tok), lambda i: (i, 0)),
        out_shape=jax.ShapeDtypeStruct((parts * rows, tok), jnp.bfloat16),
        compiler_params=pltpu.CompilerParams(vmem_limit_bytes=VMEM),
        cost_estimate=pl.CostEstimate(
            flops=2 * parts * rows * depth * cores * tok, bytes_accessed=2 * parts * rows * depth * cores, transcendentals=0
        ),
        name="project",
    )(w, ctx)


def pack_kernel(k_ref, v_ref, out_ref):
    tok, width = k_ref.shape[0], out_ref.shape[2]
    for chunk in range(out_ref.shape[0]):
        g = chunk % 8
        out_ref[chunk, :tok, :] = k_ref[:, g * width : (g + 1) * width]
        out_ref[chunk, tok:, :] = v_ref[:, g * width : (g + 1) * width]


def pack(k, v):
    tok, width = k.shape
    return pl.pallas_call(
        pack_kernel,
        out_shape=jax.ShapeDtypeStruct((16, 2 * tok, width // 8), k.dtype),
        compiler_params=pltpu.CompilerParams(vmem_limit_bytes=VMEM),
        name="pack",
    )(k, v)


def to_heads(chunks):
    return lax.all_to_all(chunks, HEAD, split_axis=0, concat_axis=0)


def to_pair(chunks):
    groups = []
    for b in range(1, N_BLK, 2):
        groups.append([c * 8 + i for c in (b, (b + 1) % N_BLK) for i in range(8)])
    return lax.all_to_all(chunks, AXES, split_axis=0, concat_axis=0, axis_index_groups=groups)


def exchange(own):
    pairs = [(b * 8 + i, (b ^ 1) * 8 + i) for b in range(N_BLK) for i in range(8)]
    return lax.ppermute(own, AXES, pairs)


def split_heads(value):
    tok = value.shape[0]
    return value.reshape(tok, 8, -1).transpose(1, 0, 2)


def local(queries, keys, values, w_out):
    tok = queries.shape[0]
    depth, cols = w_out.shape
    half = depth // 2
    here = lax.axis_index(BLK)
    ok = jnp.stack([here > 0, here < N_BLK - 1]).astype(jnp.int32)
    start = jnp.where(here % 2 == 0, 8, 0)
    kv = to_pair(pack(keys, values))

    rows = lax.all_gather(w_out.T, ("zh", "zl", "c")).reshape(2, 8, cols, depth)
    rows = lax.dynamic_slice_in_dim(rows, lax.axis_index("c") * half, half, 3)
    rows = rows.transpose(0, 2, 1, 3).reshape(2 * cols, 8 * half)
    line = lax.all_gather(rows, "y").reshape(8, 2, cols, 8 * half)
    line = line.transpose(1, 0, 2, 3).reshape(16 * cols, 8 * half)
    kv, line, queries = lax.optimization_barrier((kv, line, queries))

    weight = lax.all_gather(line, ("x", "c")).reshape(4, 2, 16 * cols, 8 * half)
    other = exchange(lax.dynamic_slice_in_dim(kv, start, 8, 0))
    q = to_heads(split_heads(queries)).reshape(8 * tok, -1)
    acc, m, l = pair_attention(ok, q, kv)
    other, acc = lax.optimization_barrier((other, acc))
    ctx = last_attention(q, other, acc, m, l, tok)
    return project(weight, to_heads(ctx)).T


def solution(mesh):
    cut = Mesh(mesh.devices.reshape(SIZES), AXES)
    return jax.shard_map(
        local,
        mesh=cut,
        in_specs=(P(AXES, None), P(AXES, None), P(AXES, None), P(HEAD, BLK)),
        out_specs=P(AXES, None),
        check_vma=False,
    )
```

```python
import functools
import math

import jax
import jax.numpy as jnp
from jax import lax
from jax.experimental import pallas as pl
from jax.experimental.pallas import tpu as pltpu
from jax.sharding import Mesh, PartitionSpec as P

HDIM = 128
LOG2E = 1.4426950408889634
FACTOR = LOG2E / math.sqrt(HDIM)
AXES = ("x", "zh", "y", "zl", "c")
SIZES = (4, 2, 8, 4, 2)
BLK = ("x", "zh", "y")
HEAD = ("zl", "c")
TILE = 256
DIMS_NT = (((1,), (1,)), ((), ()))
DIMS_TN = (((0,), (0,)), ((), ()))
VMEM = 32 * 1024 * 1024
EXTRA = 16
N_BLK = 64


def own_kernel(q_ref, k_ref, v_ref, acc_ref, m_ref, l_ref):
    scores = lax.dot_general(k_ref[...], q_ref[...], DIMS_NT, preferred_element_type=jnp.float32)
    largest = jnp.max(scores, axis=0, keepdims=True) * FACTOR
    raised = jnp.exp2(scores * FACTOR - largest)
    m_ref[0] = jnp.broadcast_to(largest, m_ref.shape[1:])
    l_ref[0] = jnp.broadcast_to(jnp.sum(raised, axis=0, keepdims=True), l_ref.shape[1:])
    acc_ref[0] = lax.dot_general(
        v_ref[...], raised.astype(jnp.bfloat16), DIMS_TN, preferred_element_type=jnp.float32
    )


def own_attention(q, k, v):
    rows, width = q.shape
    heads = width // HDIM
    return pl.pallas_call(
        own_kernel,
        grid=(heads, rows // TILE),
        in_specs=[
            pl.BlockSpec((TILE, HDIM), lambda h, i: (i, h)),
            pl.BlockSpec((rows, HDIM), lambda h, i: (0, h)),
            pl.BlockSpec((rows, HDIM), lambda h, i: (0, h)),
        ],
        out_specs=[
            pl.BlockSpec((1, HDIM, TILE), lambda h, i: (h, 0, i)),
            pl.BlockSpec((1, 8, TILE), lambda h, i: (h, 0, i)),
            pl.BlockSpec((1, 8, TILE), lambda h, i: (h, 0, i)),
        ],
        out_shape=[
            jax.ShapeDtypeStruct((heads, HDIM, rows), jnp.float32),
            jax.ShapeDtypeStruct((heads, 8, rows), jnp.float32),
            jax.ShapeDtypeStruct((heads, 8, rows), jnp.float32),
        ],
        compiler_params=pltpu.CompilerParams(vmem_limit_bytes=VMEM),
        cost_estimate=pl.CostEstimate(
            flops=rows * width, bytes_accessed=rows * width, transcendentals=0
        ),
        name="own_attention",
    )(q, k, v)


def near_kernel(ok_ref, q_ref, kp_ref, vp_ref, kn_ref, vn_ref, acc_ref, m_ref, l_ref, out_ref):
    far = jnp.float32(1e30)
    q = q_ref[...]
    m = m_ref[0][:1]
    sides = ((kp_ref, vp_ref, ok_ref[0] > 0), (kn_ref, vn_ref, ok_ref[1] > 0))
    scores = []
    for k_ref, _, ok in sides:
        s = lax.dot_general(k_ref[...], q, DIMS_NT, preferred_element_type=jnp.float32)
        scores.append(s)
        m = jnp.maximum(m, jnp.where(ok, jnp.max(s, axis=0, keepdims=True) * FACTOR, -far))
    alpha = jnp.exp2(m_ref[0][:1] - m)
    total = l_ref[0][:1] * alpha
    acc = acc_ref[0] * alpha
    for s, (_, v_ref, ok) in zip(scores, sides):
        raised = jnp.exp2(s * FACTOR - jnp.where(ok, m, far))
        total += jnp.sum(raised, axis=0, keepdims=True)
        acc += lax.dot_general(
            v_ref[...], raised.astype(jnp.bfloat16), DIMS_TN, preferred_element_type=jnp.float32
        )
    result = (acc / total).astype(jnp.bfloat16)
    tok = out_ref.shape[2]
    for part in range(out_ref.shape[0]):
        out_ref[part] = result[:, part * tok : (part + 1) * tok]


def near_attention(ok, q, kp, vp, kn, vn, acc, m, l, tok):
    rows, width = q.shape
    heads = width // HDIM
    side = pl.BlockSpec((rows, HDIM), lambda h, i: (0, h))
    row = pl.BlockSpec((1, 8, TILE), lambda h, i: (h, 0, i))
    return pl.pallas_call(
        near_kernel,
        grid=(heads, rows // TILE),
        in_specs=[
            pl.BlockSpec(memory_space=pltpu.SMEM),
            pl.BlockSpec((TILE, HDIM), lambda h, i: (i, h)),
            side,
            side,
            side,
            side,
            pl.BlockSpec((1, HDIM, TILE), lambda h, i: (h, 0, i)),
            row,
            row,
        ],
        out_specs=pl.BlockSpec((TILE // tok, HDIM, tok), lambda h, i: (i, h, 0)),
        out_shape=jax.ShapeDtypeStruct((rows // tok, width, tok), jnp.bfloat16),
        compiler_params=pltpu.CompilerParams(vmem_limit_bytes=VMEM),
        cost_estimate=pl.CostEstimate(
            flops=8 * rows * rows * width, bytes_accessed=14 * rows * width, transcendentals=2 * rows * rows * heads
        ),
        name="near_attention",
    )(ok, q, kp, vp, kn, vn, acc, m, l)


def project_kernel(mirror_ref, w_ref, ctx_ref, out_ref):
    total = None
    groups, width, tok = ctx_ref.shape
    half = width // w_ref.shape[1]
    for h in range(w_ref.shape[1]):
        ctx = jnp.concatenate(
            [ctx_ref[g ^ mirror_ref[0], h * half : (h + 1) * half, :] for g in range(groups)], axis=0
        )
        part = jnp.dot(w_ref[0, h], ctx, preferred_element_type=jnp.float32)
        total = part if total is None else total + part
    out_ref[...] = total.astype(jnp.bfloat16)


def project(mirror, w, ctx):
    parts, cores, rows, depth = w.shape
    tok = ctx.shape[2]
    return pl.pallas_call(
        project_kernel,
        grid=(parts,),
        in_specs=[
            pl.BlockSpec(memory_space=pltpu.SMEM),
            pl.BlockSpec((1, cores, rows, depth), lambda i: (i, 0, 0, 0)),
            pl.BlockSpec(ctx.shape, lambda i: (0, 0, 0)),
        ],
        out_specs=pl.BlockSpec((rows, tok), lambda i: (i, 0)),
        out_shape=jax.ShapeDtypeStruct((parts * rows, tok), jnp.bfloat16),
        compiler_params=pltpu.CompilerParams(vmem_limit_bytes=VMEM),
        cost_estimate=pl.CostEstimate(
            flops=2 * parts * rows * depth * cores * tok, bytes_accessed=2 * parts * rows * depth * cores, transcendentals=0
        ),
        name="project",
    )(mirror, w, ctx)


def columns(mirror_ref, chunk, width):
    return pl.ds(pl.multiple_of((chunk ^ mirror_ref[0]) * width, width), width)


def pack_kernel(mirror_ref, k_ref, w_ref, out_ref):
    groups, _, width = out_ref.shape
    tok = k_ref.shape[0]
    half = width // 2
    cols = w_ref.shape[0]
    for g in range(groups):
        out_ref[g, :tok, :] = k_ref[:, columns(mirror_ref, g, width)]
        part = w_ref[:, (g % 2) * half : (g % 2 + 1) * half]
        out_ref[g, tok:, :half] = part[:EXTRA]
        out_ref[g, tok:, half:] = jnp.concatenate(
            [part[EXTRA:], jnp.zeros((2 * EXTRA - cols, half), part.dtype)], axis=0
        )


def pack(mirror, k, wt):
    tok, width = k.shape[0], wt.shape[1]
    return pl.pallas_call(
        pack_kernel,
        in_specs=[pl.BlockSpec(memory_space=pltpu.SMEM)] + [pl.BlockSpec(memory_space=pltpu.VMEM)] * 2,
        out_shape=jax.ShapeDtypeStruct((8, tok + EXTRA, width), k.dtype),
        compiler_params=pltpu.CompilerParams(vmem_limit_bytes=VMEM),
        name="pack",
    )(mirror, k, wt)


def split_kernel(mirror_ref, in_ref, out_ref):
    groups, _, width = out_ref.shape
    for g in range(groups):
        out_ref[g] = in_ref[:, columns(mirror_ref, g, width)]


def split_heads(mirror, value):
    tok, width = value.shape
    return pl.pallas_call(
        split_kernel,
        in_specs=[pl.BlockSpec(memory_space=pltpu.SMEM), pl.BlockSpec(memory_space=pltpu.VMEM)],
        out_shape=jax.ShapeDtypeStruct((8, tok, width // 8), value.dtype),
        compiler_params=pltpu.CompilerParams(vmem_limit_bytes=VMEM),
        name="split_heads",
    )(mirror, value)


def unpack_kernel(in_ref, k_ref, w_ref):
    groups, tok, width = k_ref.shape
    half = width // 2
    cols = w_ref.shape[0]
    for g in range(groups):
        k_ref[g] = in_ref[g, :tok, :]
        w_ref[:EXTRA, g * half : (g + 1) * half] = in_ref[g, tok:, :half]
        w_ref[EXTRA:, g * half : (g + 1) * half] = in_ref[g, tok:, half:][: cols - EXTRA]


def unpack(moved, cols):
    groups, rows, width = moved.shape
    tok = rows - EXTRA
    return pl.pallas_call(
        unpack_kernel,
        out_shape=[
            jax.ShapeDtypeStruct((groups, tok, width), moved.dtype),
            jax.ShapeDtypeStruct((cols, groups * width // 2), moved.dtype),
        ],
        compiler_params=pltpu.CompilerParams(vmem_limit_bytes=VMEM),
        name="unpack",
    )(moved)


def to_heads(chunks):
    return lax.all_to_all(chunks, HEAD, split_axis=0, concat_axis=0)


def to_block(value, step):
    pairs = []
    for b in range(N_BLK):
        to = b + step
        if 0 <= to < N_BLK:
            turn = 6 if (b // 8) % 2 != (to // 8) % 2 else 0
            pairs += [(b * 8 + i, to * 8 + (i ^ turn)) for i in range(8)]
    return lax.ppermute(value, AXES, pairs)


def local(queries, keys, values, w_out):
    tok = queries.shape[0]
    cols, depth = w_out.shape[1], 4 * w_out.shape[0]
    here = lax.axis_index(BLK)
    ok = jnp.stack([here > 0, here < N_BLK - 1]).astype(jnp.int32)
    first = lax.axis_index("zh") == 0
    mirror = jnp.where(first, 0, 6).astype(jnp.int32)[None]
    k, w_rows = unpack(to_heads(pack(mirror, keys, w_out.T)), cols)
    k = k.reshape(8 * tok, -1)

    kp, kn = to_block(k, 1), to_block(k, -1)
    values, k = lax.optimization_barrier((values, k))
    v_chunks = split_heads(mirror, values)
    v = to_heads(v_chunks).reshape(8 * tok, -1)
    other = lax.ppermute(w_rows, "zh", [(0, 1), (1, 0)])
    pair = jnp.stack([jnp.where(first, w_rows, other), jnp.where(first, other, w_rows)])
    line = lax.all_gather(pair, "y").transpose(1, 0, 2, 3).reshape(16 * cols, depth)
    kp, kn, v, line, queries = lax.optimization_barrier((kp, kn, v, line, queries))

    weight = lax.all_gather(line, ("x", "c")).reshape(4, 2, 16 * cols, depth)
    vp, vn = to_block(v, 1), to_block(v, -1)
    q = to_heads(split_heads(mirror, queries)).reshape(8 * tok, -1)
    acc, m, l = own_attention(q, k, v)
    vp, vn, acc = lax.optimization_barrier((vp, vn, acc))
    ctx = near_attention(ok, q, kp, vp, kn, vn, acc, m, l, tok)
    return project(mirror, weight, to_heads(ctx)).T


def solution(mesh):
    cut = Mesh(mesh.devices.reshape(SIZES), AXES)
    return jax.shard_map(
        local,
        mesh=cut,
        in_specs=(P(AXES, None), P(AXES, None), P(AXES, None), P(HEAD, BLK)),
        out_specs=P(AXES, None),
        check_vma=False,
    )
```

```python
import functools
import math

import jax
import jax.numpy as jnp
from jax import lax
from jax.experimental import pallas as pl
from jax.experimental.pallas import tpu as pltpu
from jax.sharding import Mesh, PartitionSpec as P

HDIM = 128
LOG2E = 1.4426950408889634
FACTOR = LOG2E / math.sqrt(HDIM)
AXES = ("x", "zh", "y", "zl", "c")
SIZES = (4, 2, 8, 4, 2)
BLK = ("x", "zh", "y")
HEAD = ("zl", "c")
TILE = 256
DIMS_NT = (((1,), (1,)), ((), ()))
DIMS_TN = (((0,), (0,)), ((), ()))
VMEM = 32 * 1024 * 1024
EXTRA = 32
N_BLK = 64


def own_kernel(q_ref, k_ref, v_ref, acc_ref, m_ref, l_ref):
    scores = lax.dot_general(k_ref[...], q_ref[...], DIMS_NT, preferred_element_type=jnp.float32)
    largest = jnp.max(scores, axis=0, keepdims=True) * FACTOR
    raised = jnp.exp2(scores * FACTOR - largest)
    m_ref[0] = jnp.broadcast_to(largest, m_ref.shape[1:])
    l_ref[0] = jnp.broadcast_to(jnp.sum(raised, axis=0, keepdims=True), l_ref.shape[1:])
    acc_ref[0] = lax.dot_general(
        v_ref[...], raised.astype(jnp.bfloat16), DIMS_TN, preferred_element_type=jnp.float32
    )


def own_attention(q, k, v):
    rows, width = q.shape
    heads = width // HDIM
    return pl.pallas_call(
        own_kernel,
        grid=(heads, rows // TILE),
        in_specs=[
            pl.BlockSpec((TILE, HDIM), lambda h, i: (i, h)),
            pl.BlockSpec((rows, HDIM), lambda h, i: (0, h)),
            pl.BlockSpec((rows, HDIM), lambda h, i: (0, h)),
        ],
        out_specs=[
            pl.BlockSpec((1, HDIM, TILE), lambda h, i: (h, 0, i)),
            pl.BlockSpec((1, 8, TILE), lambda h, i: (h, 0, i)),
            pl.BlockSpec((1, 8, TILE), lambda h, i: (h, 0, i)),
        ],
        out_shape=[
            jax.ShapeDtypeStruct((heads, HDIM, rows), jnp.float32),
            jax.ShapeDtypeStruct((heads, 8, rows), jnp.float32),
            jax.ShapeDtypeStruct((heads, 8, rows), jnp.float32),
        ],
        compiler_params=pltpu.CompilerParams(vmem_limit_bytes=VMEM),
        cost_estimate=pl.CostEstimate(
            flops=rows * width, bytes_accessed=rows * width, transcendentals=0
        ),
        name="own_attention",
    )(q, k, v)


def near_kernel(ok_ref, q_ref, kp_ref, vp_ref, kn_ref, vn_ref, acc_ref, m_ref, l_ref, out_ref):
    far = jnp.float32(1e30)
    q = q_ref[...]
    m = m_ref[0][:1]
    sides = ((kp_ref, vp_ref, ok_ref[0] > 0), (kn_ref, vn_ref, ok_ref[1] > 0))
    scores = []
    for k_ref, _, ok in sides:
        s = lax.dot_general(k_ref[...], q, DIMS_NT, preferred_element_type=jnp.float32)
        scores.append(s)
        m = jnp.maximum(m, jnp.where(ok, jnp.max(s, axis=0, keepdims=True) * FACTOR, -far))
    alpha = jnp.exp2(m_ref[0][:1] - m)
    total = l_ref[0][:1] * alpha
    acc = acc_ref[0] * alpha
    for s, (_, v_ref, ok) in zip(scores, sides):
        raised = jnp.exp2(s * FACTOR - jnp.where(ok, m, far))
        total += jnp.sum(raised, axis=0, keepdims=True)
        acc += lax.dot_general(
            v_ref[...], raised.astype(jnp.bfloat16), DIMS_TN, preferred_element_type=jnp.float32
        )
    result = (acc / total).astype(jnp.bfloat16)
    tok = out_ref.shape[2]
    for part in range(out_ref.shape[0]):
        out_ref[part] = result[:, part * tok : (part + 1) * tok]


def near_attention(ok, q, kp, vp, kn, vn, acc, m, l, tok):
    rows, width = q.shape
    heads = width // HDIM
    side = pl.BlockSpec((rows, HDIM), lambda h, i: (0, h))
    row = pl.BlockSpec((1, 8, TILE), lambda h, i: (h, 0, i))
    return pl.pallas_call(
        near_kernel,
        grid=(heads, rows // TILE),
        in_specs=[
            pl.BlockSpec(memory_space=pltpu.SMEM),
            pl.BlockSpec((TILE, HDIM), lambda h, i: (i, h)),
            side,
            side,
            side,
            side,
            pl.BlockSpec((1, HDIM, TILE), lambda h, i: (h, 0, i)),
            row,
            row,
        ],
        out_specs=pl.BlockSpec((TILE // tok, HDIM, tok), lambda h, i: (i, h, 0)),
        out_shape=jax.ShapeDtypeStruct((rows // tok, width, tok), jnp.bfloat16),
        compiler_params=pltpu.CompilerParams(vmem_limit_bytes=VMEM),
        cost_estimate=pl.CostEstimate(
            flops=8 * rows * rows * width, bytes_accessed=14 * rows * width, transcendentals=2 * rows * rows * heads
        ),
        name="near_attention",
    )(ok, q, kp, vp, kn, vn, acc, m, l)


def project_kernel(mirror_ref, w_ref, ctx_ref, out_ref, total_ref):
    h = pl.program_id(1)
    groups, width, _ = ctx_ref.shape
    half = width // 2
    start = pl.multiple_of(h * half, half)
    ctx = jnp.concatenate([ctx_ref[g ^ mirror_ref[0], pl.ds(start, half), :] for g in range(groups)], axis=0)
    part = jnp.dot(w_ref[0, 0], ctx, preferred_element_type=jnp.float32)

    @pl.when(h == 0)
    def _():
        total_ref[...] = part

    @pl.when(h == 1)
    def _():
        out_ref[...] = (total_ref[...] + part).astype(jnp.bfloat16)


def project(mirror, w, ctx):
    parts, cores, rows, depth = w.shape
    tok = ctx.shape[2]
    return pl.pallas_call(
        project_kernel,
        grid=(parts, cores),
        in_specs=[
            pl.BlockSpec(memory_space=pltpu.SMEM),
            pl.BlockSpec((1, 1, rows, depth), lambda i, h: (i, h, 0, 0)),
            pl.BlockSpec(ctx.shape, lambda i, h: (0, 0, 0)),
        ],
        out_specs=pl.BlockSpec((rows, tok), lambda i, h: (i, 0)),
        out_shape=jax.ShapeDtypeStruct((parts * rows, tok), jnp.bfloat16),
        scratch_shapes=[pltpu.VMEM((rows, tok), jnp.float32)],
        compiler_params=pltpu.CompilerParams(vmem_limit_bytes=56 * 1024 * 1024),
        cost_estimate=pl.CostEstimate(
            flops=2 * parts * rows * depth * cores * tok, bytes_accessed=2 * parts * rows * depth * cores, transcendentals=0
        ),
        name="project",
    )(mirror, w, ctx)


def columns(mirror_ref, chunk, width):
    return pl.ds(pl.multiple_of((chunk ^ mirror_ref[0]) * width, width), width)


def choose_kernel(core_ref, in_ref, out_ref):
    groups, cols, width = in_ref.shape
    half = width // 2
    span = pl.ds(pl.multiple_of(core_ref[0] * half, half), half)
    pad = jnp.zeros((EXTRA - cols, half), out_ref.dtype)
    for g in range(groups):
        z, h = g // 8, g % 8
        out_ref[z * EXTRA : (z + 1) * EXTRA, h * half : (h + 1) * half] = jnp.concatenate(
            [in_ref[g, :, span], pad], axis=0
        )


def choose(core, rows):
    groups, _, width = rows.shape
    return pl.pallas_call(
        choose_kernel,
        in_specs=[pl.BlockSpec(memory_space=pltpu.SMEM), pl.BlockSpec(memory_space=pltpu.VMEM)],
        out_shape=jax.ShapeDtypeStruct((2 * EXTRA, groups * width // 4), rows.dtype),
        compiler_params=pltpu.CompilerParams(vmem_limit_bytes=VMEM),
        name="choose",
    )(core, rows)


def split_kernel(mirror_ref, in_ref, out_ref):
    groups, _, width = out_ref.shape
    for g in range(groups):
        out_ref[g] = in_ref[:, columns(mirror_ref, g, width)]


def split_heads(mirror, value):
    tok, width = value.shape
    return pl.pallas_call(
        split_kernel,
        in_specs=[pl.BlockSpec(memory_space=pltpu.SMEM), pl.BlockSpec(memory_space=pltpu.VMEM)],
        out_shape=jax.ShapeDtypeStruct((8, tok, width // 8), value.dtype),
        compiler_params=pltpu.CompilerParams(vmem_limit_bytes=VMEM),
        name="split_heads",
    )(mirror, value)


def tighten_kernel(cols, in_ref, out_ref):
    line = in_ref.shape[0]
    pieces = [in_ref[y, z * EXTRA : z * EXTRA + cols, :].astype(jnp.float32) for z in range(2) for y in range(line)]
    out_ref[...] = jnp.concatenate(pieces, axis=0).astype(out_ref.dtype)


def tighten(line, cols):
    count, _, depth = line.shape
    return pl.pallas_call(
        functools.partial(tighten_kernel, cols),
        out_shape=jax.ShapeDtypeStruct((2 * count * cols, depth), line.dtype),
        compiler_params=pltpu.CompilerParams(vmem_limit_bytes=VMEM),
        name="tighten",
    )(line)


def to_heads(chunks):
    return lax.all_to_all(chunks, HEAD, split_axis=0, concat_axis=0)


def to_block(value, step):
    pairs = []
    for b in range(N_BLK):
        to = b + step
        if 0 <= to < N_BLK:
            turn = 6 if (b // 8) % 2 != (to // 8) % 2 else 0
            pairs += [(b * 8 + i, to * 8 + (i ^ turn)) for i in range(8)]
    return lax.ppermute(value, AXES, pairs)


def local(queries, keys, values, w_out):
    tok = queries.shape[0]
    cols, depth = w_out.shape[1], 4 * w_out.shape[0]
    here = lax.axis_index(BLK)
    ok = jnp.stack([here > 0, here < N_BLK - 1]).astype(jnp.int32)
    first = lax.axis_index("zh") == 0
    mirror = jnp.where(first, 0, 6).astype(jnp.int32)[None]
    rows = lax.all_gather(w_out.T, ("zh", "zl", "c"))
    rows, keys = lax.optimization_barrier((rows, keys))
    w_rows = choose(lax.axis_index("c")[None], rows)
    k = to_heads(split_heads(mirror, keys)).reshape(8 * tok, -1)

    kp, kn = to_block(k, 1), to_block(k, -1)
    line = lax.all_gather(w_rows, "y")
    values, k = lax.optimization_barrier((values, k))
    v = to_heads(split_heads(mirror, values)).reshape(8 * tok, -1)
    kp, kn, v, queries, line = lax.optimization_barrier((kp, kn, v, queries, line))
    line = tighten(line, cols)
    weight = lax.all_gather(line, ("x", "c")).reshape(4, 2, 16 * cols, depth)

    vp, vn = to_block(v, 1), to_block(v, -1)
    q = to_heads(split_heads(mirror, queries)).reshape(8 * tok, -1)
    acc, m, l = own_attention(q, k, v)
    vp, vn, acc = lax.optimization_barrier((vp, vn, acc))
    ctx = near_attention(ok, q, kp, vp, kn, vn, acc, m, l, tok)
    return project(mirror, weight, to_heads(ctx)).T


def solution(mesh):
    cut = Mesh(mesh.devices.reshape(SIZES), AXES)
    return jax.shard_map(
        local,
        mesh=cut,
        in_specs=(P(AXES, None), P(AXES, None), P(AXES, None), P(HEAD, BLK)),
        out_specs=P(AXES, None),
        check_vma=False,
    )
```

```python
import functools
import math

import jax
import jax.numpy as jnp
from jax import lax
from jax.experimental import pallas as pl
from jax.experimental.pallas import tpu as pltpu
from jax.sharding import Mesh, PartitionSpec as P

HDIM = 128
LOG2E = 1.4426950408889634
FACTOR = LOG2E / math.sqrt(HDIM)
AXES = ("x", "zh", "y", "zl", "c")
SIZES = (4, 2, 8, 4, 2)
BLK = ("x", "zh", "y")
HEAD = ("zl", "c")
TILE = 1024
MIX_TILE = 1024
CHUNK = 256
PROJECT_STEP = 2
PROJECT_VMEM = 56 * 1024 * 1024
DIMS_NT = (((1,), (1,)), ((), ()))
DIMS_TN = (((0,), (0,)), ((), ()))
VMEM = 40 * 1024 * 1024
EXTRA = 32
N_BLK = 64


def score_kernel(ok_ref, q_ref, k_ref, v_ref, kp_ref, kn_ref, acc_ref, total_ref, pp_ref, pn_ref):
    far = jnp.float32(1e30)
    q = q_ref[...]
    blocks = ((k_ref, None), (kp_ref, ok_ref[0] > 0), (kn_ref, ok_ref[1] > 0))
    scores, m = [], None
    for block, (keys, ok) in enumerate(blocks):
        largest = None
        for start in range(0, keys.shape[0], CHUNK):
            s = lax.dot_general(keys[start : start + CHUNK], q, DIMS_NT, preferred_element_type=jnp.float32)
            scores.append((block, start, s))
            top = jnp.max(s, axis=0, keepdims=True)
            largest = top if largest is None else jnp.maximum(largest, top)
        largest = largest * FACTOR
        if ok is not None:
            largest = jnp.where(ok, largest, -far)
        m = largest if m is None else jnp.maximum(m, largest)
    shifts = [m if ok is None else jnp.where(ok, m, far) for _, ok in blocks]
    total, acc = jnp.zeros_like(m), None
    for block, start, s in scores:
        raised = jnp.exp2(s * FACTOR - shifts[block])
        total += jnp.sum(raised, axis=0, keepdims=True)
        probs = raised.astype(jnp.bfloat16)
        rows = slice(start, start + CHUNK)
        if block == 0:
            part = lax.dot_general(v_ref[rows], probs, DIMS_TN, preferred_element_type=jnp.float32)
            acc = part if acc is None else acc + part
        else:
            (pp_ref if block == 1 else pn_ref)[0, rows] = probs
    acc_ref[0] = acc
    total_ref[0] = jnp.broadcast_to(total, total_ref.shape[1:])


def score(ok, q, k, v, kp, kn):
    rows, width = q.shape
    heads = width // HDIM
    tile = min(TILE, rows)
    side = pl.BlockSpec((rows, HDIM), lambda h, i: (0, h))
    probs = pl.BlockSpec((1, rows, tile), lambda h, i: (h, 0, i))
    return pl.pallas_call(
        score_kernel,
        grid=(heads, rows // tile),
        in_specs=[
            pl.BlockSpec(memory_space=pltpu.SMEM),
            pl.BlockSpec((tile, HDIM), lambda h, i: (i, h)),
            side,
            side,
            side,
            side,
        ],
        out_specs=[
            pl.BlockSpec((1, HDIM, tile), lambda h, i: (h, 0, i)),
            pl.BlockSpec((1, 8, tile), lambda h, i: (h, 0, i)),
            probs,
            probs,
        ],
        out_shape=[
            jax.ShapeDtypeStruct((heads, HDIM, rows), jnp.float32),
            jax.ShapeDtypeStruct((heads, 8, rows), jnp.float32),
            jax.ShapeDtypeStruct((heads, rows, rows), jnp.bfloat16),
            jax.ShapeDtypeStruct((heads, rows, rows), jnp.bfloat16),
        ],
        compiler_params=pltpu.CompilerParams(vmem_limit_bytes=VMEM),
        cost_estimate=pl.CostEstimate(flops=rows * width, bytes_accessed=rows * width, transcendentals=0),
        name="score",
    )(ok, q, k, v, kp, kn)


def mix_kernel(pp_ref, pn_ref, vp_ref, vn_ref, acc_ref, total_ref, out_ref):
    tok = out_ref.shape[2]
    acc = acc_ref[0]
    for probs, values in ((pp_ref, vp_ref), (pn_ref, vn_ref)):
        acc += lax.dot_general(values[...], probs[0], DIMS_TN, preferred_element_type=jnp.float32)
    result = (acc / total_ref[0][:1]).astype(jnp.bfloat16)
    for part in range(out_ref.shape[0]):
        out_ref[part] = result[:, part * tok : (part + 1) * tok]


def mix(pp, pn, vp, vn, acc, total, tok):
    rows, width = vp.shape
    heads = width // HDIM
    tile = min(MIX_TILE, rows)
    side = pl.BlockSpec((rows, HDIM), lambda h, i: (0, h))
    probs = pl.BlockSpec((1, rows, tile), lambda h, i: (h, 0, i))
    return pl.pallas_call(
        mix_kernel,
        grid=(heads, rows // tile),
        in_specs=[
            probs,
            probs,
            side,
            side,
            pl.BlockSpec((1, HDIM, tile), lambda h, i: (h, 0, i)),
            pl.BlockSpec((1, 8, tile), lambda h, i: (h, 0, i)),
        ],
        out_specs=pl.BlockSpec((tile // tok, HDIM, tok), lambda h, i: (i, h, 0)),
        out_shape=jax.ShapeDtypeStruct((rows // tok, width, tok), jnp.bfloat16),
        compiler_params=pltpu.CompilerParams(vmem_limit_bytes=VMEM),
        cost_estimate=pl.CostEstimate(
            flops=4 * rows * rows * width, bytes_accessed=14 * rows * width, transcendentals=0
        ),
        name="mix",
    )(pp, pn, vp, vn, acc, total)


def project_kernel(mirror_ref, w_ref, ctx_ref, out_ref):
    groups, width, _ = ctx_ref.shape
    half = width // 2
    rows = w_ref.shape[2]
    ctx = []
    for h in range(2):
        pieces = [ctx_ref[g ^ mirror_ref[0], h * half : (h + 1) * half, :] for g in range(groups)]
        ctx.append(jnp.concatenate(pieces, axis=0))
    for part in range(w_ref.shape[0]):
        total = jnp.dot(w_ref[part, 0], ctx[0], preferred_element_type=jnp.float32)
        total += jnp.dot(w_ref[part, 1], ctx[1], preferred_element_type=jnp.float32)
        out_ref[part * rows : (part + 1) * rows] = total.astype(jnp.bfloat16)


def project(mirror, w, ctx):
    parts, halves, rows, depth = w.shape
    tok = ctx.shape[2]
    step = PROJECT_STEP
    return pl.pallas_call(
        project_kernel,
        grid=(parts // step,),
        in_specs=[
            pl.BlockSpec(memory_space=pltpu.SMEM),
            pl.BlockSpec((step, halves, rows, depth), lambda i: (i, 0, 0, 0)),
            pl.BlockSpec(ctx.shape, lambda i: (0, 0, 0)),
        ],
        out_specs=pl.BlockSpec((step * rows, tok), lambda i: (i, 0)),
        out_shape=jax.ShapeDtypeStruct((parts * rows, tok), jnp.bfloat16),
        compiler_params=pltpu.CompilerParams(vmem_limit_bytes=PROJECT_VMEM),
        cost_estimate=pl.CostEstimate(
            flops=2 * parts * rows * depth * halves * tok, bytes_accessed=2 * parts * rows * depth * halves, transcendentals=0
        ),
        name="project",
    )(mirror, w, ctx)


def columns(mirror_ref, chunk, width):
    return pl.ds(pl.multiple_of((chunk ^ mirror_ref[0]) * width, width), width)


def pack_kernel(mirror_ref, k_ref, own_ref, other_ref, out_ref):
    groups, _, width = out_ref.shape
    tok = k_ref.shape[0]
    half = width // 2
    cols = own_ref.shape[0]
    first = mirror_ref[0] == 0
    pad = jnp.zeros((EXTRA - cols, width), out_ref.dtype)
    own, other = own_ref[...].astype(jnp.float32), other_ref[...].astype(jnp.float32)
    low = jnp.where(first, own, other).astype(out_ref.dtype)
    high = jnp.where(first, other, own).astype(out_ref.dtype)
    below = []
    for c in range(2):
        span = slice(c * half, (c + 1) * half)
        below.append(jnp.concatenate([jnp.concatenate([low[:, span], high[:, span]], axis=1), pad], axis=0))
    for g in range(groups):
        out_ref[g, :tok, :] = k_ref[:, columns(mirror_ref, g, width)]
        out_ref[g, tok:, :] = below[g % 2]


def pack(mirror, k, own, other):
    tok, width = k.shape[0], own.shape[1]
    return pl.pallas_call(
        pack_kernel,
        in_specs=[pl.BlockSpec(memory_space=pltpu.SMEM)] + [pl.BlockSpec(memory_space=pltpu.VMEM)] * 3,
        out_shape=jax.ShapeDtypeStruct((8, tok + EXTRA, width), k.dtype),
        compiler_params=pltpu.CompilerParams(vmem_limit_bytes=VMEM),
        name="pack",
    )(mirror, k, own, other)


def split_kernel(mirror_ref, in_ref, out_ref):
    groups, _, width = out_ref.shape
    for g in range(groups):
        out_ref[g] = in_ref[:, columns(mirror_ref, g, width)]


def split_heads(mirror, value):
    tok, width = value.shape
    return pl.pallas_call(
        split_kernel,
        in_specs=[pl.BlockSpec(memory_space=pltpu.SMEM), pl.BlockSpec(memory_space=pltpu.VMEM)],
        out_shape=jax.ShapeDtypeStruct((8, tok, width // 8), value.dtype),
        compiler_params=pltpu.CompilerParams(vmem_limit_bytes=VMEM),
        name="split_heads",
    )(mirror, value)


def unpack_kernel(in_ref, k_ref, w_ref):
    groups, tok, width = k_ref.shape
    half = width // 2
    for g in range(groups):
        k_ref[g] = in_ref[g, :tok, :]
        for z in range(2):
            w_ref[z * EXTRA : (z + 1) * EXTRA, g * half : (g + 1) * half] = in_ref[
                g, tok:, z * half : (z + 1) * half
            ]


def unpack(moved):
    groups, rows, width = moved.shape
    tok = rows - EXTRA
    return pl.pallas_call(
        unpack_kernel,
        out_shape=[
            jax.ShapeDtypeStruct((groups, tok, width), moved.dtype),
            jax.ShapeDtypeStruct((2 * EXTRA, groups * width // 2), moved.dtype),
        ],
        compiler_params=pltpu.CompilerParams(vmem_limit_bytes=VMEM),
        name="unpack",
    )(moved)


def tighten_kernel(cols, in_ref, out_ref):
    line = in_ref.shape[0]
    pieces = [in_ref[y, z * EXTRA : z * EXTRA + cols, :].astype(jnp.float32) for z in range(2) for y in range(line)]
    out_ref[...] = jnp.concatenate(pieces, axis=0).astype(out_ref.dtype)


def tighten(line, cols):
    count, _, depth = line.shape
    return pl.pallas_call(
        functools.partial(tighten_kernel, cols),
        out_shape=jax.ShapeDtypeStruct((2 * count * cols, depth), line.dtype),
        compiler_params=pltpu.CompilerParams(vmem_limit_bytes=VMEM),
        name="tighten",
    )(line)


def to_heads(chunks):
    return lax.all_to_all(chunks, HEAD, split_axis=0, concat_axis=0)


def to_block(value, step):
    pairs = []
    for b in range(N_BLK):
        to = b + step
        if 0 <= to < N_BLK:
            turn = 6 if (b // 8) % 2 != (to // 8) % 2 else 0
            pairs += [(b * 8 + i, to * 8 + (i ^ turn)) for i in range(8)]
    return lax.ppermute(value, AXES, pairs)


def local(queries, keys, values, w_out):
    tok = queries.shape[0]
    cols, depth = w_out.shape[1], 4 * w_out.shape[0]
    here = lax.axis_index(BLK)
    ok = jnp.stack([here > 0, here < N_BLK - 1]).astype(jnp.int32)
    first = lax.axis_index("zh") == 0
    mirror = jnp.where(first, 0, 6).astype(jnp.int32)[None]
    own_w = w_out.T
    other_w = lax.ppermute(own_w, "zh", [(0, 1), (1, 0)])
    k, w_rows = unpack(to_heads(pack(mirror, keys, own_w, other_w)))
    k = k.reshape(8 * tok, -1)

    kp, kn = to_block(k, 1), to_block(k, -1)
    line = lax.all_gather(w_rows, "y")
    values, k = lax.optimization_barrier((values, k))
    v = to_heads(split_heads(mirror, values)).reshape(8 * tok, -1)
    kp, kn, v, queries, line = lax.optimization_barrier((kp, kn, v, queries, line))
    line = tighten(line, cols)
    weight = lax.all_gather(line, ("x", "c")).reshape(4, 2, 16 * cols, depth)

    vp, vn = to_block(v, 1), to_block(v, -1)
    q = to_heads(split_heads(mirror, queries)).reshape(8 * tok, -1)
    acc, total, pp, pn = score(ok, q, k, v, kp, kn)
    vp, vn, acc = lax.optimization_barrier((vp, vn, acc))
    ctx = mix(pp, pn, vp, vn, acc, total, tok)
    return project(mirror, weight, to_heads(ctx)).T


def solution(mesh):
    cut = Mesh(mesh.devices.reshape(SIZES), AXES)
    return jax.shard_map(
        local,
        mesh=cut,
        in_specs=(P(AXES, None), P(AXES, None), P(AXES, None), P(HEAD, BLK)),
        out_specs=P(AXES, None),
        check_vma=False,
    )
```

```python
import functools
import math

import jax
import jax.numpy as jnp
from jax import lax
from jax.experimental import pallas as pl
from jax.experimental.pallas import tpu as pltpu
from jax.sharding import Mesh, PartitionSpec as P

HDIM = 128
LOG2E = 1.4426950408889634
FACTOR = LOG2E / math.sqrt(HDIM)
AXES = ("x", "zh", "y", "zl", "c")
SIZES = (4, 2, 8, 4, 2)
BLK = ("x", "zh", "y")
HEAD = ("zl", "c")
TILE = 1024
MIX_TILE = 1024
CHUNK = 256
PROJECT_STEP = 4
PROJECT_VMEM = 56 * 1024 * 1024
DIMS_NT = (((1,), (1,)), ((), ()))
DIMS_TN = (((0,), (0,)), ((), ()))
VMEM = 40 * 1024 * 1024
EXTRA = 16
N_BLK = 64


def score_kernel(ok_ref, q_ref, k_ref, v_ref, kp_ref, kn_ref, acc_ref, total_ref, pp_ref, pn_ref):
    far = jnp.float32(1e30)
    q = q_ref[...]
    blocks = ((k_ref, None), (kp_ref, ok_ref[0] > 0), (kn_ref, ok_ref[1] > 0))
    scores, m = [], None
    for block, (keys, ok) in enumerate(blocks):
        largest = None
        for start in range(0, keys.shape[0], CHUNK):
            s = lax.dot_general(keys[start : start + CHUNK], q, DIMS_NT, preferred_element_type=jnp.float32)
            scores.append((block, start, s))
            top = jnp.max(s, axis=0, keepdims=True)
            largest = top if largest is None else jnp.maximum(largest, top)
        largest = largest * FACTOR
        if ok is not None:
            largest = jnp.where(ok, largest, -far)
        m = largest if m is None else jnp.maximum(m, largest)
    shifts = [m if ok is None else jnp.where(ok, m, far) for _, ok in blocks]
    total, acc = jnp.zeros_like(m), None
    for block, start, s in scores:
        raised = jnp.exp2(s * FACTOR - shifts[block])
        total += jnp.sum(raised, axis=0, keepdims=True)
        probs = raised.astype(jnp.bfloat16)
        rows = slice(start, start + CHUNK)
        if block == 0:
            part = lax.dot_general(v_ref[rows], probs, DIMS_TN, preferred_element_type=jnp.float32)
            acc = part if acc is None else acc + part
        else:
            (pp_ref if block == 1 else pn_ref)[0, rows] = probs
    acc_ref[0] = acc
    total_ref[0] = jnp.broadcast_to(total, total_ref.shape[1:])


def score(ok, q, k, v, kp, kn):
    rows, width = q.shape
    heads = width // HDIM
    tile = min(TILE, rows)
    side = pl.BlockSpec((rows, HDIM), lambda h, i: (0, h))
    probs = pl.BlockSpec((1, rows, tile), lambda h, i: (h, 0, i))
    return pl.pallas_call(
        score_kernel,
        grid=(heads, rows // tile),
        in_specs=[
            pl.BlockSpec(memory_space=pltpu.SMEM),
            pl.BlockSpec((tile, HDIM), lambda h, i: (i, h)),
            side,
            side,
            side,
            side,
        ],
        out_specs=[
            pl.BlockSpec((1, HDIM, tile), lambda h, i: (h, 0, i)),
            pl.BlockSpec((1, 8, tile), lambda h, i: (h, 0, i)),
            probs,
            probs,
        ],
        out_shape=[
            jax.ShapeDtypeStruct((heads, HDIM, rows), jnp.float32),
            jax.ShapeDtypeStruct((heads, 8, rows), jnp.float32),
            jax.ShapeDtypeStruct((heads, rows, rows), jnp.bfloat16),
            jax.ShapeDtypeStruct((heads, rows, rows), jnp.bfloat16),
        ],
        compiler_params=pltpu.CompilerParams(vmem_limit_bytes=VMEM),
        cost_estimate=pl.CostEstimate(flops=rows * width, bytes_accessed=rows * width, transcendentals=0),
        name="score",
    )(ok, q, k, v, kp, kn)


def mix_kernel(pp_ref, pn_ref, vp_ref, vn_ref, acc_ref, total_ref, out_ref):
    tok = out_ref.shape[2]
    acc = acc_ref[0]
    for probs, values in ((pp_ref, vp_ref), (pn_ref, vn_ref)):
        acc += lax.dot_general(values[...], probs[0], DIMS_TN, preferred_element_type=jnp.float32)
    result = (acc / total_ref[0][:1]).astype(jnp.bfloat16)
    for part in range(out_ref.shape[0]):
        out_ref[part] = result[:, part * tok : (part + 1) * tok]


def mix(pp, pn, vp, vn, acc, total, tok):
    rows, width = vp.shape
    heads = width // HDIM
    tile = min(MIX_TILE, rows)
    side = pl.BlockSpec((rows, HDIM), lambda h, i: (0, h))
    probs = pl.BlockSpec((1, rows, tile), lambda h, i: (h, 0, i))
    return pl.pallas_call(
        mix_kernel,
        grid=(heads, rows // tile),
        in_specs=[
            probs,
            probs,
            side,
            side,
            pl.BlockSpec((1, HDIM, tile), lambda h, i: (h, 0, i)),
            pl.BlockSpec((1, 8, tile), lambda h, i: (h, 0, i)),
        ],
        out_specs=pl.BlockSpec((tile // tok, HDIM, tok), lambda h, i: (i, h, 0)),
        out_shape=jax.ShapeDtypeStruct((rows // tok, width, tok), jnp.bfloat16),
        compiler_params=pltpu.CompilerParams(vmem_limit_bytes=VMEM),
        cost_estimate=pl.CostEstimate(
            flops=4 * rows * rows * width, bytes_accessed=14 * rows * width, transcendentals=0
        ),
        name="mix",
    )(pp, pn, vp, vn, acc, total)


def project_kernel(cols, mirror_ref, w_ref, ctx_ref, out_ref, total_ref):
    step = pl.program_id(0)
    groups, width, _ = ctx_ref.shape
    half = width // 2
    lines, _, rows, _ = w_ref.shape
    ctx = []
    for h in range(2):
        pieces = [ctx_ref[g ^ mirror_ref[0], h * half : (h + 1) * half, :] for g in range(groups)]
        ctx.append(jnp.concatenate(pieces, axis=0))
    for part in range(lines):
        total = jnp.dot(w_ref[part, 0], ctx[0], preferred_element_type=jnp.float32)
        total += jnp.dot(w_ref[part, 1], ctx[1], preferred_element_type=jnp.float32)
        total_ref[step * lines + part] = total

    @pl.when(step == pl.num_programs(0) - 1)
    def _():
        pieces = []
        for outer in range(rows // cols):
            for y in range(total_ref.shape[0]):
                pieces.append(total_ref[y, outer * cols : (outer + 1) * cols, :])
        out_ref[...] = jnp.concatenate(pieces, axis=0).astype(jnp.bfloat16)


def project(mirror, w, ctx, cols):
    count, halves, rows, depth = w.shape
    tok = ctx.shape[2]
    step = PROJECT_STEP
    return pl.pallas_call(
        functools.partial(project_kernel, cols),
        grid=(count // step,),
        in_specs=[
            pl.BlockSpec(memory_space=pltpu.SMEM),
            pl.BlockSpec((step, halves, rows, depth), lambda i: (i, 0, 0, 0)),
            pl.BlockSpec(ctx.shape, lambda i: (0, 0, 0)),
        ],
        out_specs=pl.BlockSpec((count * rows, tok), lambda i: (0, 0)),
        out_shape=jax.ShapeDtypeStruct((count * rows, tok), jnp.bfloat16),
        scratch_shapes=[pltpu.VMEM((count, rows, tok), jnp.float32)],
        compiler_params=pltpu.CompilerParams(vmem_limit_bytes=PROJECT_VMEM),
        cost_estimate=pl.CostEstimate(
            flops=2 * count * rows * depth * halves * tok, bytes_accessed=2 * count * rows * depth * halves, transcendentals=0
        ),
        name="project",
    )(mirror, w, ctx)


def columns(mirror_ref, chunk, width):
    return pl.ds(pl.multiple_of((chunk ^ mirror_ref[0]) * width, width), width)


def pack_kernel(mirror_ref, k_ref, w_ref, out_ref):
    groups, _, width = out_ref.shape
    tok = k_ref.shape[0]
    half = width // 2
    cols = w_ref.shape[0]
    for g in range(groups):
        out_ref[g, :tok, :] = k_ref[:, columns(mirror_ref, g, width)]
        part = w_ref[:, (g % 2) * half : (g % 2 + 1) * half]
        out_ref[g, tok:, :half] = part[:EXTRA]
        out_ref[g, tok:, half:] = jnp.concatenate(
            [part[EXTRA:], jnp.zeros((2 * EXTRA - cols, half), part.dtype)], axis=0
        )


def pack(mirror, k, wt):
    tok, width = k.shape[0], wt.shape[1]
    return pl.pallas_call(
        pack_kernel,
        in_specs=[pl.BlockSpec(memory_space=pltpu.SMEM)] + [pl.BlockSpec(memory_space=pltpu.VMEM)] * 2,
        out_shape=jax.ShapeDtypeStruct((8, tok + EXTRA, width), k.dtype),
        compiler_params=pltpu.CompilerParams(vmem_limit_bytes=VMEM),
        name="pack",
    )(mirror, k, wt)


def split_kernel(mirror_ref, in_ref, out_ref):
    groups, _, width = out_ref.shape
    for g in range(groups):
        out_ref[g] = in_ref[:, columns(mirror_ref, g, width)]


def split_heads(mirror, value):
    tok, width = value.shape
    return pl.pallas_call(
        split_kernel,
        in_specs=[pl.BlockSpec(memory_space=pltpu.SMEM), pl.BlockSpec(memory_space=pltpu.VMEM)],
        out_shape=jax.ShapeDtypeStruct((8, tok, width // 8), value.dtype),
        compiler_params=pltpu.CompilerParams(vmem_limit_bytes=VMEM),
        name="split_heads",
    )(mirror, value)


def unpack_kernel(in_ref, k_ref, w_ref):
    groups, tok, width = k_ref.shape
    half = width // 2
    for g in range(groups):
        k_ref[g] = in_ref[g, :tok, :]
        w_ref[:EXTRA, g * half : (g + 1) * half] = in_ref[g, tok:, :half]
        w_ref[EXTRA:, g * half : (g + 1) * half] = in_ref[g, tok:, half:]


def unpack(moved):
    groups, rows, width = moved.shape
    tok = rows - EXTRA
    return pl.pallas_call(
        unpack_kernel,
        out_shape=[
            jax.ShapeDtypeStruct((groups, tok, width), moved.dtype),
            jax.ShapeDtypeStruct((2 * EXTRA, groups * width // 2), moved.dtype),
        ],
        compiler_params=pltpu.CompilerParams(vmem_limit_bytes=VMEM),
        name="unpack",
    )(moved)


def tighten_kernel(cols, in_ref, out_ref):
    rows = 2 * EXTRA
    pieces = []
    for x in range(in_ref.shape[0]):
        for z in range(2):
            pieces.append(in_ref[x, z * rows : z * rows + cols, :].astype(jnp.float32))
    out_ref[...] = jnp.concatenate(pieces, axis=0).astype(out_ref.dtype)


def tighten(line, cols):
    count, _, depth = line.shape
    return pl.pallas_call(
        functools.partial(tighten_kernel, cols),
        out_shape=jax.ShapeDtypeStruct((2 * count * cols, depth), line.dtype),
        compiler_params=pltpu.CompilerParams(vmem_limit_bytes=VMEM),
        name="tighten",
    )(line)


def to_heads(chunks):
    return lax.all_to_all(chunks, HEAD, split_axis=0, concat_axis=0)


def to_block(value, step):
    pairs = []
    for b in range(N_BLK):
        to = b + step
        if 0 <= to < N_BLK:
            turn = 6 if (b // 8) % 2 != (to // 8) % 2 else 0
            pairs += [(b * 8 + i, to * 8 + (i ^ turn)) for i in range(8)]
    return lax.ppermute(value, AXES, pairs)


def local(queries, keys, values, w_out):
    tok = queries.shape[0]
    cols, depth = w_out.shape[1], 4 * w_out.shape[0]
    here = lax.axis_index(BLK)
    ok = jnp.stack([here > 0, here < N_BLK - 1]).astype(jnp.int32)
    first = lax.axis_index("zh") == 0
    mirror = jnp.where(first, 0, 6).astype(jnp.int32)[None]
    k, w_rows = unpack(to_heads(pack(mirror, keys, w_out.T)))
    k = k.reshape(8 * tok, -1)

    kp, kn = to_block(k, 1), to_block(k, -1)
    values, k = lax.optimization_barrier((values, k))
    v = to_heads(split_heads(mirror, values)).reshape(8 * tok, -1)
    other = lax.ppermute(w_rows, "zh", [(0, 1), (1, 0)])
    pair = jnp.concatenate([jnp.where(first, w_rows, other), jnp.where(first, other, w_rows)])
    line = tighten(lax.all_gather(pair, "x"), cols)
    kp, kn, v, line, queries = lax.optimization_barrier((kp, kn, v, line, queries))

    weight = lax.all_gather(line, ("y", "c")).reshape(8, 2, 8 * cols, depth)
    vp, vn = to_block(v, 1), to_block(v, -1)
    q = to_heads(split_heads(mirror, queries)).reshape(8 * tok, -1)
    acc, total, pp, pn = score(ok, q, k, v, kp, kn)
    vp, vn, acc = lax.optimization_barrier((vp, vn, acc))
    ctx = mix(pp, pn, vp, vn, acc, total, tok)
    return project(mirror, weight, to_heads(ctx), cols).T


def solution(mesh):
    cut = Mesh(mesh.devices.reshape(SIZES), AXES)
    return jax.shard_map(
        local,
        mesh=cut,
        in_specs=(P(AXES, None), P(AXES, None), P(AXES, None), P(HEAD, BLK)),
        out_specs=P(AXES, None),
        check_vma=False,
    )
```

```python
import functools
import math

import jax
import jax.numpy as jnp
from jax import lax
from jax.experimental import pallas as pl
from jax.experimental.pallas import tpu as pltpu
from jax.sharding import Mesh, PartitionSpec as P

HDIM = 128
LOG2E = 1.4426950408889634
FACTOR = LOG2E / math.sqrt(HDIM)
AXES = ("x", "zh", "y", "zl", "c")
SIZES = (4, 2, 8, 4, 2)
BLK = ("x", "zh", "y")
HEAD = ("zl", "c")
TILE = 1024
MIX_TILE = 1024
CHUNK = 256
PROJECT_STEP = 4
PROJECT_VMEM = 56 * 1024 * 1024
DIMS_NT = (((1,), (1,)), ((), ()))
DIMS_TN = (((0,), (0,)), ((), ()))
VMEM = 40 * 1024 * 1024
EXTRA = 16
N_BLK = 64


def score_kernel(ok_ref, q_ref, k_ref, v_ref, kp_ref, kn_ref, acc_ref, total_ref, pp_ref, pn_ref):
    far = jnp.float32(1e30)
    chunks, tok, _ = q_ref.shape
    q = q_ref[...].reshape(chunks * tok, HDIM)
    own = v_ref[...].reshape(chunks * tok, HDIM)
    blocks = ((k_ref, None), (kp_ref, ok_ref[0] > 0), (kn_ref, ok_ref[1] > 0))
    scores, m = [], None
    for block, (keys, ok) in enumerate(blocks):
        largest = None
        for start in range(0, keys.shape[0], CHUNK):
            s = lax.dot_general(keys[start : start + CHUNK], q, DIMS_NT, preferred_element_type=jnp.float32)
            scores.append((block, start, s))
            top = jnp.max(s, axis=0, keepdims=True)
            largest = top if largest is None else jnp.maximum(largest, top)
        largest = largest * FACTOR
        if ok is not None:
            largest = jnp.where(ok, largest, -far)
        m = largest if m is None else jnp.maximum(m, largest)
    shifts = [m if ok is None else jnp.where(ok, m, far) for _, ok in blocks]
    total, acc = jnp.zeros_like(m), None
    for block, start, s in scores:
        raised = jnp.exp2(s * FACTOR - shifts[block])
        total += jnp.sum(raised, axis=0, keepdims=True)
        probs = raised.astype(jnp.bfloat16)
        rows = slice(start, start + CHUNK)
        if block == 0:
            part = lax.dot_general(own[rows], probs, DIMS_TN, preferred_element_type=jnp.float32)
            acc = part if acc is None else acc + part
        else:
            (pp_ref if block == 1 else pn_ref)[0, rows] = probs
    acc_ref[0] = acc
    total_ref[0] = jnp.broadcast_to(total, total_ref.shape[1:])


def score(ok, vq, k, kp, kn):
    rows, width = k.shape
    heads = width // HDIM
    joint = (vq.shape[0], vq.shape[1] // 2, HDIM)
    side = pl.BlockSpec((rows, HDIM), lambda h: (0, h))
    probs = pl.BlockSpec((1, rows, rows), lambda h: (h, 0, 0))
    return pl.pallas_call(
        score_kernel,
        grid=(heads,),
        in_specs=[
            pl.BlockSpec(memory_space=pltpu.SMEM),
            pl.BlockSpec(joint, lambda h: (0, 1, h)),
            side,
            pl.BlockSpec(joint, lambda h: (0, 0, h)),
            side,
            side,
        ],
        out_specs=[
            pl.BlockSpec((1, HDIM, rows), lambda h: (h, 0, 0)),
            pl.BlockSpec((1, 8, rows), lambda h: (h, 0, 0)),
            probs,
            probs,
        ],
        out_shape=[
            jax.ShapeDtypeStruct((heads, HDIM, rows), jnp.float32),
            jax.ShapeDtypeStruct((heads, 8, rows), jnp.float32),
            jax.ShapeDtypeStruct((heads, rows, rows), jnp.bfloat16),
            jax.ShapeDtypeStruct((heads, rows, rows), jnp.bfloat16),
        ],
        compiler_params=pltpu.CompilerParams(vmem_limit_bytes=VMEM),
        cost_estimate=pl.CostEstimate(flops=rows * width, bytes_accessed=rows * width, transcendentals=0),
        name="score",
    )(ok, vq, k, vq, kp, kn)


def mix_kernel(pp_ref, pn_ref, vp_ref, vn_ref, acc_ref, total_ref, out_ref):
    tok = out_ref.shape[2]
    acc = acc_ref[0]
    for probs, values in ((pp_ref, vp_ref), (pn_ref, vn_ref)):
        acc += lax.dot_general(values[...], probs[0], DIMS_TN, preferred_element_type=jnp.float32)
    result = (acc / total_ref[0][:1]).astype(jnp.bfloat16)
    for part in range(out_ref.shape[0]):
        out_ref[part] = result[:, part * tok : (part + 1) * tok]


def mix(pp, pn, vp, vn, acc, total, tok):
    rows, width = vp.shape
    heads = width // HDIM
    tile = min(MIX_TILE, rows)
    side = pl.BlockSpec((rows, HDIM), lambda h, i: (0, h))
    probs = pl.BlockSpec((1, rows, tile), lambda h, i: (h, 0, i))
    return pl.pallas_call(
        mix_kernel,
        grid=(heads, rows // tile),
        in_specs=[
            probs,
            probs,
            side,
            side,
            pl.BlockSpec((1, HDIM, tile), lambda h, i: (h, 0, i)),
            pl.BlockSpec((1, 8, tile), lambda h, i: (h, 0, i)),
        ],
        out_specs=pl.BlockSpec((tile // tok, HDIM, tok), lambda h, i: (i, h, 0)),
        out_shape=jax.ShapeDtypeStruct((rows // tok, width, tok), jnp.bfloat16),
        compiler_params=pltpu.CompilerParams(vmem_limit_bytes=VMEM),
        cost_estimate=pl.CostEstimate(
            flops=4 * rows * rows * width, bytes_accessed=14 * rows * width, transcendentals=0
        ),
        name="mix",
    )(pp, pn, vp, vn, acc, total)


def project_kernel(cols, mirror_ref, w_ref, ctx_ref, out_ref, total_ref):
    step = pl.program_id(0)
    groups, width, _ = ctx_ref.shape
    half = width // 2
    lines, _, rows, _ = w_ref.shape
    ctx = []
    for h in range(2):
        pieces = [ctx_ref[g ^ mirror_ref[0], h * half : (h + 1) * half, :] for g in range(groups)]
        ctx.append(jnp.concatenate(pieces, axis=0))
    for part in range(lines):
        total = jnp.dot(w_ref[part, 0], ctx[0], preferred_element_type=jnp.float32)
        total += jnp.dot(w_ref[part, 1], ctx[1], preferred_element_type=jnp.float32)
        total_ref[step * lines + part] = total

    @pl.when(step == pl.num_programs(0) - 1)
    def _():
        pieces = []
        for outer in range(rows // cols):
            for y in range(total_ref.shape[0]):
                pieces.append(total_ref[y, outer * cols : (outer + 1) * cols, :])
        out_ref[...] = jnp.concatenate(pieces, axis=0).astype(jnp.bfloat16)


def project(mirror, w, ctx, cols):
    count, halves, rows, depth = w.shape
    tok = ctx.shape[2]
    step = PROJECT_STEP
    return pl.pallas_call(
        functools.partial(project_kernel, cols),
        grid=(count // step,),
        in_specs=[
            pl.BlockSpec(memory_space=pltpu.SMEM),
            pl.BlockSpec((step, halves, rows, depth), lambda i: (i, 0, 0, 0)),
            pl.BlockSpec(ctx.shape, lambda i: (0, 0, 0)),
        ],
        out_specs=pl.BlockSpec((count * rows, tok), lambda i: (0, 0)),
        out_shape=jax.ShapeDtypeStruct((count * rows, tok), jnp.bfloat16),
        scratch_shapes=[pltpu.VMEM((count, rows, tok), jnp.float32)],
        compiler_params=pltpu.CompilerParams(vmem_limit_bytes=PROJECT_VMEM),
        cost_estimate=pl.CostEstimate(
            flops=2 * count * rows * depth * halves * tok, bytes_accessed=2 * count * rows * depth * halves, transcendentals=0
        ),
        name="project",
    )(mirror, w, ctx)


def columns(mirror_ref, chunk, width):
    return pl.ds(pl.multiple_of((chunk ^ mirror_ref[0]) * width, width), width)


def pack_kernel(mirror_ref, k_ref, w_ref, out_ref):
    groups, _, width = out_ref.shape
    tok = k_ref.shape[0]
    half = width // 2
    cols = w_ref.shape[0]
    for g in range(groups):
        out_ref[g, :tok, :] = k_ref[:, columns(mirror_ref, g, width)]
        part = w_ref[:, (g % 2) * half : (g % 2 + 1) * half]
        out_ref[g, tok:, :half] = part[:EXTRA]
        out_ref[g, tok:, half:] = jnp.concatenate(
            [part[EXTRA:], jnp.zeros((2 * EXTRA - cols, half), part.dtype)], axis=0
        )


def pack(mirror, k, wt):
    tok, width = k.shape[0], wt.shape[1]
    return pl.pallas_call(
        pack_kernel,
        in_specs=[pl.BlockSpec(memory_space=pltpu.SMEM)] + [pl.BlockSpec(memory_space=pltpu.VMEM)] * 2,
        out_shape=jax.ShapeDtypeStruct((8, tok + EXTRA, width), k.dtype),
        compiler_params=pltpu.CompilerParams(vmem_limit_bytes=VMEM),
        name="pack",
    )(mirror, k, wt)


def join_kernel(mirror_ref, v_ref, q_ref, out_ref):
    groups, rows, width = out_ref.shape
    tok = rows // 2
    for g in range(groups):
        out_ref[g, :tok, :] = v_ref[:, columns(mirror_ref, g, width)]
        out_ref[g, tok:, :] = q_ref[:, columns(mirror_ref, g, width)]


def join_heads(mirror, v, q):
    tok, width = v.shape
    return pl.pallas_call(
        join_kernel,
        in_specs=[pl.BlockSpec(memory_space=pltpu.SMEM)] + [pl.BlockSpec(memory_space=pltpu.VMEM)] * 2,
        out_shape=jax.ShapeDtypeStruct((8, 2 * tok, width // 8), v.dtype),
        compiler_params=pltpu.CompilerParams(vmem_limit_bytes=VMEM),
        name="join_heads",
    )(mirror, v, q)


def unpack_kernel(in_ref, k_ref, w_ref):
    groups, tok, width = k_ref.shape
    half = width // 2
    for g in range(groups):
        k_ref[g] = in_ref[g, :tok, :]
        w_ref[:EXTRA, g * half : (g + 1) * half] = in_ref[g, tok:, :half]
        w_ref[EXTRA:, g * half : (g + 1) * half] = in_ref[g, tok:, half:]


def unpack(moved):
    groups, rows, width = moved.shape
    tok = rows - EXTRA
    return pl.pallas_call(
        unpack_kernel,
        out_shape=[
            jax.ShapeDtypeStruct((groups, tok, width), moved.dtype),
            jax.ShapeDtypeStruct((2 * EXTRA, groups * width // 2), moved.dtype),
        ],
        compiler_params=pltpu.CompilerParams(vmem_limit_bytes=VMEM),
        name="unpack",
    )(moved)


def tighten_kernel(cols, in_ref, out_ref):
    rows = 2 * EXTRA
    pieces = []
    for x in range(in_ref.shape[0]):
        for z in range(2):
            pieces.append(in_ref[x, z * rows : z * rows + cols, :].astype(jnp.float32))
    out_ref[...] = jnp.concatenate(pieces, axis=0).astype(out_ref.dtype)


def tighten(line, cols):
    count, _, depth = line.shape
    return pl.pallas_call(
        functools.partial(tighten_kernel, cols),
        out_shape=jax.ShapeDtypeStruct((2 * count * cols, depth), line.dtype),
        compiler_params=pltpu.CompilerParams(vmem_limit_bytes=VMEM),
        name="tighten",
    )(line)


def to_heads(chunks):
    return lax.all_to_all(chunks, HEAD, split_axis=0, concat_axis=0)


def to_block(value, step):
    pairs = []
    for b in range(N_BLK):
        to = b + step
        if 0 <= to < N_BLK:
            turn = 6 if (b // 8) % 2 != (to // 8) % 2 else 0
            pairs += [(b * 8 + i, to * 8 + (i ^ turn)) for i in range(8)]
    return lax.ppermute(value, AXES, pairs)


def local(queries, keys, values, w_out):
    tok = queries.shape[0]
    cols, depth = w_out.shape[1], 4 * w_out.shape[0]
    here = lax.axis_index(BLK)
    ok = jnp.stack([here > 0, here < N_BLK - 1]).astype(jnp.int32)
    first = lax.axis_index("zh") == 0
    mirror = jnp.where(first, 0, 6).astype(jnp.int32)[None]
    k, w_rows = unpack(to_heads(pack(mirror, keys, w_out.T)))
    k = k.reshape(8 * tok, -1)

    kp, kn = to_block(k, 1), to_block(k, -1)
    values, k = lax.optimization_barrier((values, k))
    vq = to_heads(join_heads(mirror, values, queries))
    other = lax.ppermute(w_rows, "zh", [(0, 1), (1, 0)])
    pair = jnp.concatenate([jnp.where(first, w_rows, other), jnp.where(first, other, w_rows)])
    line = tighten(lax.all_gather(pair, "x"), cols)
    kp, kn, vq, line = lax.optimization_barrier((kp, kn, vq, line))

    v = vq[:, :tok].reshape(8 * tok, -1)
    vp, vn = to_block(v, 1), to_block(v, -1)
    weight = lax.all_gather(line, ("y", "c")).reshape(8, 2, 8 * cols, depth)
    acc, total, pp, pn = score(ok, vq, k, kp, kn)
    vp, vn, acc = lax.optimization_barrier((vp, vn, acc))
    ctx = mix(pp, pn, vp, vn, acc, total, tok)
    return project(mirror, weight, to_heads(ctx), cols).T


def solution(mesh):
    cut = Mesh(mesh.devices.reshape(SIZES), AXES)
    return jax.shard_map(
        local,
        mesh=cut,
        in_specs=(P(AXES, None), P(AXES, None), P(AXES, None), P(HEAD, BLK)),
        out_specs=P(AXES, None),
        check_vma=False,
    )
```

```python
import functools
import math

import jax
import jax.numpy as jnp
from jax import lax
from jax.experimental import pallas as pl
from jax.experimental.pallas import tpu as pltpu
from jax.sharding import Mesh, PartitionSpec as P

HDIM = 128
LOG2E = 1.4426950408889634
FACTOR = LOG2E / math.sqrt(HDIM)
AXES = ("x", "zh", "y", "zl", "c")
SIZES = (4, 2, 8, 4, 2)
BLK = ("x", "zh", "y")
HEAD = ("zl", "c")
TILE = 1024
MIX_TILE = 1024
CHUNK = 256
PROJECT_STEP = 4
PROJECT_VMEM = 56 * 1024 * 1024
DIMS_NT = (((1,), (1,)), ((), ()))
DIMS_TN = (((0,), (0,)), ((), ()))
VMEM = 40 * 1024 * 1024
EXTRA = 16
N_BLK = 64


def score_kernel(ok_ref, q_ref, k_ref, v_ref, kp_ref, kn_ref, acc_ref, total_ref, pp_ref, pn_ref):
    far = jnp.float32(1e30)
    chunks, tok, _ = q_ref.shape
    q = q_ref[...].reshape(chunks * tok, HDIM)
    own = v_ref[...].reshape(chunks * tok, HDIM)
    blocks = ((k_ref, None), (kp_ref, ok_ref[0] > 0), (kn_ref, ok_ref[1] > 0))
    scores, m = [], None
    for block, (keys, ok) in enumerate(blocks):
        largest = None
        for start in range(0, keys.shape[0], CHUNK):
            s = lax.dot_general(keys[start : start + CHUNK], q, DIMS_NT, preferred_element_type=jnp.float32)
            scores.append((block, start, s))
            top = jnp.max(s, axis=0, keepdims=True)
            largest = top if largest is None else jnp.maximum(largest, top)
        largest = largest * FACTOR
        if ok is not None:
            largest = jnp.where(ok, largest, -far)
        m = largest if m is None else jnp.maximum(m, largest)
    shifts = [m if ok is None else jnp.where(ok, m, far) for _, ok in blocks]
    total, acc = jnp.zeros_like(m), None
    for block, start, s in scores:
        raised = jnp.exp2(s * FACTOR - shifts[block])
        total += jnp.sum(raised, axis=0, keepdims=True)
        probs = raised.astype(jnp.bfloat16)
        rows = slice(start, start + CHUNK)
        if block == 0:
            part = lax.dot_general(own[rows], probs, DIMS_TN, preferred_element_type=jnp.float32)
            acc = part if acc is None else acc + part
        else:
            (pp_ref if block == 1 else pn_ref)[0, rows] = probs
    acc_ref[0] = acc
    total_ref[0] = jnp.broadcast_to(total, total_ref.shape[1:])


def score(ok, vq, k, kp, kn):
    rows, width = k.shape
    heads = width // HDIM
    joint = (vq.shape[0], vq.shape[1] // 2, HDIM)
    side = pl.BlockSpec((rows, HDIM), lambda h: (0, h))
    probs = pl.BlockSpec((1, rows, rows), lambda h: (h, 0, 0))
    return pl.pallas_call(
        score_kernel,
        grid=(heads,),
        in_specs=[
            pl.BlockSpec(memory_space=pltpu.SMEM),
            pl.BlockSpec(joint, lambda h: (0, 1, h)),
            side,
            pl.BlockSpec(joint, lambda h: (0, 0, h)),
            side,
            side,
        ],
        out_specs=[
            pl.BlockSpec((1, HDIM, rows), lambda h: (h, 0, 0)),
            pl.BlockSpec((1, 8, rows), lambda h: (h, 0, 0)),
            probs,
            probs,
        ],
        out_shape=[
            jax.ShapeDtypeStruct((heads, HDIM, rows), jnp.float32),
            jax.ShapeDtypeStruct((heads, 8, rows), jnp.float32),
            jax.ShapeDtypeStruct((heads, rows, rows), jnp.bfloat16),
            jax.ShapeDtypeStruct((heads, rows, rows), jnp.bfloat16),
        ],
        compiler_params=pltpu.CompilerParams(vmem_limit_bytes=VMEM),
        cost_estimate=pl.CostEstimate(flops=rows * width, bytes_accessed=rows * width, transcendentals=0),
        name="score",
    )(ok, vq, k, vq, kp, kn)


def mix_kernel(pp_ref, pn_ref, vp_ref, vn_ref, acc_ref, total_ref, out_ref):
    tok = out_ref.shape[2]
    acc = acc_ref[0]
    for probs, values in ((pp_ref, vp_ref), (pn_ref, vn_ref)):
        acc += lax.dot_general(values[...], probs[0], DIMS_TN, preferred_element_type=jnp.float32)
    result = (acc / total_ref[0][:1]).astype(jnp.bfloat16)
    for part in range(out_ref.shape[0]):
        out_ref[part] = result[:, part * tok : (part + 1) * tok]


def mix(pp, pn, vp, vn, acc, total, tok):
    rows, width = vp.shape
    heads = width // HDIM
    tile = min(MIX_TILE, rows)
    side = pl.BlockSpec((rows, HDIM), lambda h, i: (0, h))
    probs = pl.BlockSpec((1, rows, tile), lambda h, i: (h, 0, i))
    return pl.pallas_call(
        mix_kernel,
        grid=(heads, rows // tile),
        in_specs=[
            probs,
            probs,
            side,
            side,
            pl.BlockSpec((1, HDIM, tile), lambda h, i: (h, 0, i)),
            pl.BlockSpec((1, 8, tile), lambda h, i: (h, 0, i)),
        ],
        out_specs=pl.BlockSpec((tile // tok, HDIM, tok), lambda h, i: (i, h, 0)),
        out_shape=jax.ShapeDtypeStruct((rows // tok, width, tok), jnp.bfloat16),
        compiler_params=pltpu.CompilerParams(vmem_limit_bytes=VMEM),
        cost_estimate=pl.CostEstimate(
            flops=4 * rows * rows * width, bytes_accessed=14 * rows * width, transcendentals=0
        ),
        name="mix",
    )(pp, pn, vp, vn, acc, total)


def project_kernel(cols, mirror_ref, w_ref, ctx_ref, out_ref, total_ref):
    step = pl.program_id(0)
    groups, width, _ = ctx_ref.shape
    half = width // 2
    lines, _, rows, _ = w_ref.shape
    ctx = []
    for h in range(2):
        pieces = [ctx_ref[g ^ mirror_ref[0], h * half : (h + 1) * half, :] for g in range(groups)]
        ctx.append(jnp.concatenate(pieces, axis=0))
    for part in range(lines):
        total = jnp.dot(w_ref[part, 0], ctx[0], preferred_element_type=jnp.float32)
        total += jnp.dot(w_ref[part, 1], ctx[1], preferred_element_type=jnp.float32)
        total_ref[step * lines + part] = total

    @pl.when(step == pl.num_programs(0) - 1)
    def _():
        pieces = []
        for outer in range(rows // cols):
            for y in range(total_ref.shape[0]):
                pieces.append(total_ref[y, outer * cols : (outer + 1) * cols, :])
        out_ref[...] = jnp.concatenate(pieces, axis=0).astype(jnp.bfloat16)


def project(mirror, w, ctx, cols):
    count, halves, rows, depth = w.shape
    tok = ctx.shape[2]
    step = PROJECT_STEP
    return pl.pallas_call(
        functools.partial(project_kernel, cols),
        grid=(count // step,),
        in_specs=[
            pl.BlockSpec(memory_space=pltpu.SMEM),
            pl.BlockSpec((step, halves, rows, depth), lambda i: (i, 0, 0, 0)),
            pl.BlockSpec(ctx.shape, lambda i: (0, 0, 0)),
        ],
        out_specs=pl.BlockSpec((count * rows, tok), lambda i: (0, 0)),
        out_shape=jax.ShapeDtypeStruct((count * rows, tok), jnp.bfloat16),
        scratch_shapes=[pltpu.VMEM((count, rows, tok), jnp.float32)],
        compiler_params=pltpu.CompilerParams(vmem_limit_bytes=PROJECT_VMEM),
        cost_estimate=pl.CostEstimate(
            flops=2 * count * rows * depth * halves * tok, bytes_accessed=2 * count * rows * depth * halves, transcendentals=0
        ),
        name="project",
    )(mirror, w, ctx)


def columns(mirror_ref, chunk, width):
    return pl.ds(pl.multiple_of((chunk ^ mirror_ref[0]) * width, width), width)


def pack_kernel(mirror_ref, k_ref, w_ref, out_ref):
    groups, _, width = out_ref.shape
    tok = k_ref.shape[0]
    half = width // 2
    cols = w_ref.shape[0]
    for g in range(groups):
        out_ref[g, :tok, :] = k_ref[:, columns(mirror_ref, g, width)]
        part = w_ref[:, (g % 2) * half : (g % 2 + 1) * half]
        out_ref[g, tok:, :half] = part[:EXTRA]
        out_ref[g, tok:, half:] = jnp.concatenate(
            [part[EXTRA:], jnp.zeros((2 * EXTRA - cols, half), part.dtype)], axis=0
        )


def pack(mirror, k, wt):
    tok, width = k.shape[0], wt.shape[1]
    return pl.pallas_call(
        pack_kernel,
        in_specs=[pl.BlockSpec(memory_space=pltpu.SMEM)] + [pl.BlockSpec(memory_space=pltpu.VMEM)] * 2,
        out_shape=jax.ShapeDtypeStruct((8, tok + EXTRA, width), k.dtype),
        compiler_params=pltpu.CompilerParams(vmem_limit_bytes=VMEM),
        name="pack",
    )(mirror, k, wt)


def join_kernel(mirror_ref, v_ref, q_ref, out_ref):
    groups, rows, width = out_ref.shape
    tok = rows // 2
    for g in range(groups):
        out_ref[g, :tok, :] = v_ref[:, columns(mirror_ref, g, width)]
        out_ref[g, tok:, :] = q_ref[:, columns(mirror_ref, g, width)]


def join_heads(mirror, v, q):
    tok, width = v.shape
    return pl.pallas_call(
        join_kernel,
        in_specs=[pl.BlockSpec(memory_space=pltpu.SMEM)] + [pl.BlockSpec(memory_space=pltpu.VMEM)] * 2,
        out_shape=jax.ShapeDtypeStruct((8, 2 * tok, width // 8), v.dtype),
        compiler_params=pltpu.CompilerParams(vmem_limit_bytes=VMEM),
        name="join_heads",
    )(mirror, v, q)


def unpack_kernel(in_ref, k_ref, w_ref):
    groups, tok, width = k_ref.shape
    half = width // 2
    for g in range(groups):
        k_ref[g] = in_ref[g, :tok, :]
        w_ref[:EXTRA, g * half : (g + 1) * half] = in_ref[g, tok:, :half]
        w_ref[EXTRA:, g * half : (g + 1) * half] = in_ref[g, tok:, half:]


def unpack(moved):
    groups, rows, width = moved.shape
    tok = rows - EXTRA
    return pl.pallas_call(
        unpack_kernel,
        out_shape=[
            jax.ShapeDtypeStruct((groups, tok, width), moved.dtype),
            jax.ShapeDtypeStruct((2 * EXTRA, groups * width // 2), moved.dtype),
        ],
        compiler_params=pltpu.CompilerParams(vmem_limit_bytes=VMEM),
        name="unpack",
    )(moved)


def tighten_kernel(cols, in_ref, out_ref):
    rows = 2 * EXTRA
    pieces = []
    for x in range(in_ref.shape[0]):
        for z in range(2):
            pieces.append(in_ref[x, z * rows : z * rows + cols, :].astype(jnp.float32))
    out_ref[...] = jnp.concatenate(pieces, axis=0).astype(out_ref.dtype)


def tighten(line, cols):
    count, _, depth = line.shape
    return pl.pallas_call(
        functools.partial(tighten_kernel, cols),
        out_shape=jax.ShapeDtypeStruct((2 * count * cols, depth), line.dtype),
        compiler_params=pltpu.CompilerParams(vmem_limit_bytes=VMEM),
        name="tighten",
    )(line)


def to_heads(chunks):
    return lax.all_to_all(chunks, HEAD, split_axis=0, concat_axis=0)


def to_block(value, step):
    pairs = []
    for b in range(N_BLK):
        to = b + step
        if 0 <= to < N_BLK:
            turn = 6 if (b // 8) % 2 != (to // 8) % 2 else 0
            pairs += [(b * 8 + i, to * 8 + (i ^ turn)) for i in range(8)]
    return lax.ppermute(value, AXES, pairs)


def local(queries, keys, values, w_out):
    tok = queries.shape[0]
    cols, depth = w_out.shape[1], 4 * w_out.shape[0]
    here = lax.axis_index(BLK)
    ok = jnp.stack([here > 0, here < N_BLK - 1]).astype(jnp.int32)
    first = lax.axis_index("zh") == 0
    mirror = jnp.where(first, 0, 6).astype(jnp.int32)[None]
    k, w_rows = unpack(to_heads(pack(mirror, keys, w_out.T)))
    k = k.reshape(8 * tok, -1)

    kp, kn = to_block(k, 1), to_block(k, -1)
    other = lax.ppermute(w_rows, "zh", [(0, 1), (1, 0)])
    values, other = lax.optimization_barrier((values, other))
    vq = to_heads(join_heads(mirror, values, queries))
    pair = jnp.concatenate([jnp.where(first, w_rows, other), jnp.where(first, other, w_rows)])
    line = tighten(lax.all_gather(pair, "x"), cols)
    kp, kn, vq, line = lax.optimization_barrier((kp, kn, vq, line))

    v = vq[:, :tok].reshape(8 * tok, -1)
    vp, vn = to_block(v, 1), to_block(v, -1)
    weight = lax.all_gather(line, ("y", "c")).reshape(8, 2, 8 * cols, depth)
    acc, total, pp, pn = score(ok, vq, k, kp, kn)
    vp, vn, acc = lax.optimization_barrier((vp, vn, acc))
    ctx = mix(pp, pn, vp, vn, acc, total, tok)
    return project(mirror, weight, to_heads(ctx), cols).T


def solution(mesh):
    cut = Mesh(mesh.devices.reshape(SIZES), AXES)
    return jax.shard_map(
        local,
        mesh=cut,
        in_specs=(P(AXES, None), P(AXES, None), P(AXES, None), P(HEAD, BLK)),
        out_specs=P(AXES, None),
        check_vma=False,
    )
```

```python
import functools
import math

import jax
import jax.numpy as jnp
from jax import lax
from jax.experimental import pallas as pl
from jax.experimental.pallas import tpu as pltpu
from jax.sharding import Mesh, PartitionSpec as P

HDIM = 128
LOG2E = 1.4426950408889634
FACTOR = LOG2E / math.sqrt(HDIM)
AXES = ("x", "zh", "y", "zl", "c")
SIZES = (4, 2, 8, 4, 2)
BLK = ("x", "zh", "y")
HEAD = ("zl", "c")
TILE = 1024
MIX_TILE = 1024
CHUNK = 256
PROJECT_STEP = 4
HINT = 28_750_000_000
PROJECT_VMEM = 56 * 1024 * 1024
DIMS_NT = (((1,), (1,)), ((), ()))
DIMS_TN = (((0,), (0,)), ((), ()))
VMEM = 40 * 1024 * 1024
EXTRA = 16
N_BLK = 64


def score_kernel(ok_ref, q_ref, k_ref, v_ref, kp_ref, kn_ref, acc_ref, total_ref, pp_ref, pn_ref):
    far = jnp.float32(1e30)
    chunks, tok, _ = q_ref.shape
    q = q_ref[...].reshape(chunks * tok, HDIM)
    own = v_ref[...].reshape(chunks * tok, HDIM)
    blocks = ((k_ref, None), (kp_ref, ok_ref[0] > 0), (kn_ref, ok_ref[1] > 0))
    scores, m = [], None
    for block, (keys, ok) in enumerate(blocks):
        largest = None
        for start in range(0, keys.shape[0], CHUNK):
            s = lax.dot_general(keys[start : start + CHUNK], q, DIMS_NT, preferred_element_type=jnp.float32)
            scores.append((block, start, s))
            top = jnp.max(s, axis=0, keepdims=True)
            largest = top if largest is None else jnp.maximum(largest, top)
        largest = largest * FACTOR
        if ok is not None:
            largest = jnp.where(ok, largest, -far)
        m = largest if m is None else jnp.maximum(m, largest)
    shifts = [m if ok is None else jnp.where(ok, m, far) for _, ok in blocks]
    total, acc = jnp.zeros_like(m), None
    for block, start, s in scores:
        raised = jnp.exp2(s * FACTOR - shifts[block])
        total += jnp.sum(raised, axis=0, keepdims=True)
        probs = raised.astype(jnp.bfloat16)
        rows = slice(start, start + CHUNK)
        if block == 0:
            part = lax.dot_general(own[rows], probs, DIMS_TN, preferred_element_type=jnp.float32)
            acc = part if acc is None else acc + part
        else:
            (pp_ref if block == 1 else pn_ref)[0, rows] = probs
    acc_ref[0] = acc
    total_ref[0] = jnp.broadcast_to(total, total_ref.shape[1:])


def score(ok, vq, k, kp, kn):
    rows, width = k.shape
    heads = width // HDIM
    joint = (vq.shape[0], vq.shape[1] // 2, HDIM)
    side = pl.BlockSpec((rows, HDIM), lambda h: (0, h))
    probs = pl.BlockSpec((1, rows, rows), lambda h: (h, 0, 0))
    return pl.pallas_call(
        score_kernel,
        grid=(heads,),
        in_specs=[
            pl.BlockSpec(memory_space=pltpu.SMEM),
            pl.BlockSpec(joint, lambda h: (0, 1, h)),
            side,
            pl.BlockSpec(joint, lambda h: (0, 0, h)),
            side,
            side,
        ],
        out_specs=[
            pl.BlockSpec((1, HDIM, rows), lambda h: (h, 0, 0)),
            pl.BlockSpec((1, 8, rows), lambda h: (h, 0, 0)),
            probs,
            probs,
        ],
        out_shape=[
            jax.ShapeDtypeStruct((heads, HDIM, rows), jnp.float32),
            jax.ShapeDtypeStruct((heads, 8, rows), jnp.float32),
            jax.ShapeDtypeStruct((heads, rows, rows), jnp.bfloat16),
            jax.ShapeDtypeStruct((heads, rows, rows), jnp.bfloat16),
        ],
        compiler_params=pltpu.CompilerParams(vmem_limit_bytes=VMEM),
        cost_estimate=pl.CostEstimate(flops=rows * width, bytes_accessed=rows * width, transcendentals=0),
        name="score",
    )(ok, vq, k, vq, kp, kn)


def mix_kernel(pp_ref, pn_ref, vp_ref, vn_ref, acc_ref, total_ref, out_ref):
    tok = out_ref.shape[2]
    acc = acc_ref[0]
    for probs, values in ((pp_ref, vp_ref), (pn_ref, vn_ref)):
        acc += lax.dot_general(values[...], probs[0], DIMS_TN, preferred_element_type=jnp.float32)
    result = (acc / total_ref[0][:1]).astype(jnp.bfloat16)
    for part in range(out_ref.shape[0]):
        out_ref[part] = result[:, part * tok : (part + 1) * tok]


def mix(pp, pn, vp, vn, acc, total, tok):
    rows, width = vp.shape
    heads = width // HDIM
    tile = min(MIX_TILE, rows)
    side = pl.BlockSpec((rows, HDIM), lambda h, i: (0, h))
    probs = pl.BlockSpec((1, rows, tile), lambda h, i: (h, 0, i))
    return pl.pallas_call(
        mix_kernel,
        grid=(heads, rows // tile),
        in_specs=[
            probs,
            probs,
            side,
            side,
            pl.BlockSpec((1, HDIM, tile), lambda h, i: (h, 0, i)),
            pl.BlockSpec((1, 8, tile), lambda h, i: (h, 0, i)),
        ],
        out_specs=pl.BlockSpec((tile // tok, HDIM, tok), lambda h, i: (i, h, 0)),
        out_shape=jax.ShapeDtypeStruct((rows // tok, width, tok), jnp.bfloat16),
        compiler_params=pltpu.CompilerParams(vmem_limit_bytes=VMEM),
        cost_estimate=pl.CostEstimate(
            flops=4 * rows * rows * width, bytes_accessed=14 * rows * width, transcendentals=0
        ),
        name="mix",
    )(pp, pn, vp, vn, acc, total)


def project_kernel(cols, mirror_ref, w_ref, ctx_ref, out_ref, total_ref):
    step = pl.program_id(0)
    groups, width, _ = ctx_ref.shape
    half = width // 2
    lines, _, rows, _ = w_ref.shape
    ctx = []
    for h in range(2):
        pieces = [ctx_ref[g ^ mirror_ref[0], h * half : (h + 1) * half, :] for g in range(groups)]
        ctx.append(jnp.concatenate(pieces, axis=0))
    for part in range(lines):
        total = jnp.dot(w_ref[part, 0], ctx[0], preferred_element_type=jnp.float32)
        total += jnp.dot(w_ref[part, 1], ctx[1], preferred_element_type=jnp.float32)
        total_ref[step * lines + part] = total

    @pl.when(step == pl.num_programs(0) - 1)
    def _():
        pieces = []
        for outer in range(rows // cols):
            for y in range(total_ref.shape[0]):
                pieces.append(total_ref[y, outer * cols : (outer + 1) * cols, :])
        out_ref[...] = jnp.concatenate(pieces, axis=0).astype(jnp.bfloat16)


def project(mirror, w, ctx, cols):
    count, halves, rows, depth = w.shape
    tok = ctx.shape[2]
    step = PROJECT_STEP
    return pl.pallas_call(
        functools.partial(project_kernel, cols),
        grid=(count // step,),
        in_specs=[
            pl.BlockSpec(memory_space=pltpu.SMEM),
            pl.BlockSpec((step, halves, rows, depth), lambda i: (i, 0, 0, 0)),
            pl.BlockSpec(ctx.shape, lambda i: (0, 0, 0)),
        ],
        out_specs=pl.BlockSpec((count * rows, tok), lambda i: (0, 0)),
        out_shape=jax.ShapeDtypeStruct((count * rows, tok), jnp.bfloat16),
        scratch_shapes=[pltpu.VMEM((count, rows, tok), jnp.float32)],
        compiler_params=pltpu.CompilerParams(vmem_limit_bytes=PROJECT_VMEM),
        cost_estimate=pl.CostEstimate(
            flops=2 * count * rows * depth * halves * tok, bytes_accessed=2 * count * rows * depth * halves, transcendentals=0
        ),
        name="project",
    )(mirror, w, ctx)


def columns(mirror_ref, chunk, width):
    return pl.ds(pl.multiple_of((chunk ^ mirror_ref[0]) * width, width), width)


def pack_kernel(mirror_ref, k_ref, w_ref, out_ref):
    groups, _, width = out_ref.shape
    tok = k_ref.shape[0]
    half = width // 2
    cols = w_ref.shape[0]
    for g in range(groups):
        out_ref[g, :tok, :] = k_ref[:, columns(mirror_ref, g, width)]
        part = w_ref[:, (g % 2) * half : (g % 2 + 1) * half]
        out_ref[g, tok:, :half] = part[:EXTRA]
        out_ref[g, tok:, half:] = jnp.concatenate(
            [part[EXTRA:], jnp.zeros((2 * EXTRA - cols, half), part.dtype)], axis=0
        )


def pack(mirror, k, wt):
    tok, width = k.shape[0], wt.shape[1]
    return pl.pallas_call(
        pack_kernel,
        in_specs=[pl.BlockSpec(memory_space=pltpu.SMEM)] + [pl.BlockSpec(memory_space=pltpu.VMEM)] * 2,
        out_shape=jax.ShapeDtypeStruct((8, tok + EXTRA, width), k.dtype),
        compiler_params=pltpu.CompilerParams(vmem_limit_bytes=VMEM),
        name="pack",
    )(mirror, k, wt)


def join_kernel(mirror_ref, v_ref, q_ref, out_ref):
    groups, rows, width = out_ref.shape
    tok = rows // 2
    for g in range(groups):
        out_ref[g, :tok, :] = v_ref[:, columns(mirror_ref, g, width)]
        out_ref[g, tok:, :] = q_ref[:, columns(mirror_ref, g, width)]


def join_heads(mirror, v, q):
    tok, width = v.shape
    return pl.pallas_call(
        join_kernel,
        in_specs=[pl.BlockSpec(memory_space=pltpu.SMEM)] + [pl.BlockSpec(memory_space=pltpu.VMEM)] * 2,
        out_shape=jax.ShapeDtypeStruct((8, 2 * tok, width // 8), v.dtype),
        compiler_params=pltpu.CompilerParams(vmem_limit_bytes=VMEM),
        name="join_heads",
    )(mirror, v, q)


def unpack_kernel(in_ref, k_ref, w_ref):
    groups, tok, width = k_ref.shape
    half = width // 2
    for g in range(groups):
        k_ref[g] = in_ref[g, :tok, :]
        w_ref[:EXTRA, g * half : (g + 1) * half] = in_ref[g, tok:, :half]
        w_ref[EXTRA:, g * half : (g + 1) * half] = in_ref[g, tok:, half:]


def unpack(moved):
    groups, rows, width = moved.shape
    tok = rows - EXTRA
    return pl.pallas_call(
        unpack_kernel,
        out_shape=[
            jax.ShapeDtypeStruct((groups, tok, width), moved.dtype),
            jax.ShapeDtypeStruct((2 * EXTRA, groups * width // 2), moved.dtype),
        ],
        compiler_params=pltpu.CompilerParams(vmem_limit_bytes=VMEM),
        name="unpack",
    )(moved)


def tighten_kernel(cols, in_ref, out_ref):
    rows = 2 * EXTRA
    pieces = []
    for x in range(in_ref.shape[0]):
        for z in range(2):
            pieces.append(in_ref[x, z * rows : z * rows + cols, :].astype(jnp.float32))
    out_ref[...] = jnp.concatenate(pieces, axis=0).astype(out_ref.dtype)


def tighten(line, cols):
    count, _, depth = line.shape
    return pl.pallas_call(
        functools.partial(tighten_kernel, cols),
        out_shape=jax.ShapeDtypeStruct((2 * count * cols, depth), line.dtype),
        compiler_params=pltpu.CompilerParams(vmem_limit_bytes=VMEM),
        name="tighten",
    )(line)


def to_heads(chunks):
    return lax.all_to_all(chunks, HEAD, split_axis=0, concat_axis=0)


def behind_kernel(ok_ref, kp_ref, kn_ref, out_ref):
    for side in range(2):
        out_ref[side] = ok_ref[side]


def behind(ok, kp, kn):
    return pl.pallas_call(
        behind_kernel,
        in_specs=[pl.BlockSpec(memory_space=pltpu.SMEM)] + [pl.BlockSpec(memory_space=pl.ANY)] * 2,
        out_specs=pl.BlockSpec(memory_space=pltpu.SMEM),
        out_shape=jax.ShapeDtypeStruct(ok.shape, ok.dtype),
        cost_estimate=pl.CostEstimate(flops=HINT, bytes_accessed=0, transcendentals=0),
        name="behind",
    )(ok, kp, kn)


def to_block(value, step):
    pairs = []
    for b in range(N_BLK):
        to = b + step
        if 0 <= to < N_BLK:
            turn = 6 if (b // 8) % 2 != (to // 8) % 2 else 0
            pairs += [(b * 8 + i, to * 8 + (i ^ turn)) for i in range(8)]
    return lax.ppermute(value, AXES, pairs)


def local(queries, keys, values, w_out):
    tok = queries.shape[0]
    cols, depth = w_out.shape[1], 4 * w_out.shape[0]
    here = lax.axis_index(BLK)
    ok = jnp.stack([here > 0, here < N_BLK - 1]).astype(jnp.int32)
    first = lax.axis_index("zh") == 0
    mirror = jnp.where(first, 0, 6).astype(jnp.int32)[None]
    k, w_rows = unpack(to_heads(pack(mirror, keys, w_out.T)))
    k = k.reshape(8 * tok, -1)

    kp, kn = to_block(k, 1), to_block(k, -1)
    values, k = lax.optimization_barrier((values, k))
    vq = to_heads(join_heads(mirror, values, queries))
    other = lax.ppermute(w_rows, "zh", [(0, 1), (1, 0)])
    pair = jnp.concatenate([jnp.where(first, w_rows, other), jnp.where(first, other, w_rows)])
    line = tighten(lax.all_gather(pair, "x"), cols)
    ok = behind(ok, kp, kn)
    ok, vq, line = lax.optimization_barrier((ok, vq, line))

    v = vq[:, :tok].reshape(8 * tok, -1)
    vp, vn = to_block(v, 1), to_block(v, -1)
    weight = lax.all_gather(line, ("y", "c")).reshape(8, 2, 8 * cols, depth)
    acc, total, pp, pn = score(ok, vq, k, kp, kn)
    vp, vn, acc = lax.optimization_barrier((vp, vn, acc))
    ctx = mix(pp, pn, vp, vn, acc, total, tok)
    return project(mirror, weight, to_heads(ctx), cols).T


def solution(mesh):
    cut = Mesh(mesh.devices.reshape(SIZES), AXES)
    return jax.shard_map(
        local,
        mesh=cut,
        in_specs=(P(AXES, None), P(AXES, None), P(AXES, None), P(HEAD, BLK)),
        out_specs=P(AXES, None),
        check_vma=False,
    )
```

```python
import functools
import math

import jax
import jax.numpy as jnp
from jax import lax
from jax.experimental import pallas as pl
from jax.experimental.pallas import tpu as pltpu
from jax.sharding import Mesh, PartitionSpec as P

HDIM = 128
LOG2E = 1.4426950408889634
FACTOR = LOG2E / math.sqrt(HDIM)
AXES = ("x", "zh", "y", "zl", "c")
SIZES = (4, 2, 8, 4, 2)
BLK = ("x", "zh", "y")
HEAD = ("zl", "c")
TILE = 1024
MIX_TILE = 1024
CHUNK = 256
PROJECT_STEP = 4
HINT = 28_750_000_000
HINT_LAST = 9_200_000_000
PROJECT_VMEM = 56 * 1024 * 1024
DIMS_NT = (((1,), (1,)), ((), ()))
DIMS_TN = (((0,), (0,)), ((), ()))
VMEM = 40 * 1024 * 1024
EXTRA = 16
N_BLK = 64


def score_kernel(ok_ref, q_ref, k_ref, v_ref, kp_ref, kn_ref, acc_ref, total_ref, pp_ref, pn_ref):
    far = jnp.float32(1e30)
    chunks, tok, _ = q_ref.shape
    q = q_ref[...].reshape(chunks * tok, HDIM)
    own = v_ref[...].reshape(chunks * tok, HDIM)
    blocks = ((k_ref, None), (kp_ref, ok_ref[0] > 0), (kn_ref, ok_ref[1] > 0))
    scores, m = [], None
    for block, (keys, ok) in enumerate(blocks):
        largest = None
        for start in range(0, keys.shape[0], CHUNK):
            s = lax.dot_general(keys[start : start + CHUNK], q, DIMS_NT, preferred_element_type=jnp.float32)
            scores.append((block, start, s))
            top = jnp.max(s, axis=0, keepdims=True)
            largest = top if largest is None else jnp.maximum(largest, top)
        largest = largest * FACTOR
        if ok is not None:
            largest = jnp.where(ok, largest, -far)
        m = largest if m is None else jnp.maximum(m, largest)
    shifts = [m if ok is None else jnp.where(ok, m, far) for _, ok in blocks]
    total, acc = jnp.zeros_like(m), None
    for block, start, s in scores:
        raised = jnp.exp2(s * FACTOR - shifts[block])
        total += jnp.sum(raised, axis=0, keepdims=True)
        probs = raised.astype(jnp.bfloat16)
        rows = slice(start, start + CHUNK)
        if block == 0:
            part = lax.dot_general(own[rows], probs, DIMS_TN, preferred_element_type=jnp.float32)
            acc = part if acc is None else acc + part
        else:
            (pp_ref if block == 1 else pn_ref)[0, rows] = probs
    acc_ref[0] = acc
    total_ref[0] = jnp.broadcast_to(total, total_ref.shape[1:])


def score(ok, vq, k, kp, kn):
    rows, width = k.shape
    heads = width // HDIM
    joint = (vq.shape[0], vq.shape[1] // 2, HDIM)
    side = pl.BlockSpec((rows, HDIM), lambda h: (0, h))
    probs = pl.BlockSpec((1, rows, rows), lambda h: (h, 0, 0))
    return pl.pallas_call(
        score_kernel,
        grid=(heads,),
        in_specs=[
            pl.BlockSpec(memory_space=pltpu.SMEM),
            pl.BlockSpec(joint, lambda h: (0, 1, h)),
            side,
            pl.BlockSpec(joint, lambda h: (0, 0, h)),
            side,
            side,
        ],
        out_specs=[
            pl.BlockSpec((1, HDIM, rows), lambda h: (h, 0, 0)),
            pl.BlockSpec((1, 8, rows), lambda h: (h, 0, 0)),
            probs,
            probs,
        ],
        out_shape=[
            jax.ShapeDtypeStruct((heads, HDIM, rows), jnp.float32),
            jax.ShapeDtypeStruct((heads, 8, rows), jnp.float32),
            jax.ShapeDtypeStruct((heads, rows, rows), jnp.bfloat16),
            jax.ShapeDtypeStruct((heads, rows, rows), jnp.bfloat16),
        ],
        compiler_params=pltpu.CompilerParams(vmem_limit_bytes=VMEM),
        cost_estimate=pl.CostEstimate(flops=rows * width, bytes_accessed=rows * width, transcendentals=0),
        name="score",
    )(ok, vq, k, vq, kp, kn)


def mix_kernel(ok_ref, pp_ref, pn_ref, vp_ref, vn_ref, acc_ref, total_ref, out_ref):
    tok = out_ref.shape[2]
    acc = acc_ref[0]
    for probs, values in ((pp_ref, vp_ref), (pn_ref, vn_ref)):
        acc += lax.dot_general(values[...], probs[0], DIMS_TN, preferred_element_type=jnp.float32)
    result = (acc / total_ref[0][:1]).astype(jnp.bfloat16)
    for part in range(out_ref.shape[0]):
        out_ref[part] = result[:, part * tok : (part + 1) * tok]


def mix(head, ok, pp, pn, vp, vn, acc, total, tok):
    rows = vp.shape[0]
    side = pl.BlockSpec((rows, HDIM), lambda i: (0, 0))
    probs = pl.BlockSpec((1, rows, rows), lambda i: (head, 0, 0))
    return pl.pallas_call(
        mix_kernel,
        grid=(1,),
        in_specs=[
            pl.BlockSpec(memory_space=pltpu.SMEM),
            probs,
            probs,
            side,
            side,
            pl.BlockSpec((1, HDIM, rows), lambda i: (head, 0, 0)),
            pl.BlockSpec((1, 8, rows), lambda i: (head, 0, 0)),
        ],
        out_specs=pl.BlockSpec((rows // tok, HDIM, tok), lambda i: (0, 0, 0)),
        out_shape=jax.ShapeDtypeStruct((rows // tok, HDIM, tok), jnp.bfloat16),
        compiler_params=pltpu.CompilerParams(vmem_limit_bytes=VMEM),
        cost_estimate=pl.CostEstimate(
            flops=4 * rows * rows * HDIM, bytes_accessed=14 * rows * HDIM, transcendentals=0
        ),
        name="mix",
    )(ok, pp, pn, vp, vn, acc, total)


def gathered(mirror_ref, ctx_ref):
    return jnp.concatenate([ctx_ref[g ^ mirror_ref[0]] for g in range(ctx_ref.shape[0])], axis=0)


def project_first_kernel(mirror_ref, w_ref, ctx_ref, total_ref):
    ctx = gathered(mirror_ref, ctx_ref)
    for part in range(w_ref.shape[0]):
        total_ref[part] = jnp.dot(w_ref[part, 0], ctx, preferred_element_type=jnp.float32)


def project_last_kernel(cols, mirror_ref, w_ref, ctx_ref, first_ref, out_ref, total_ref):
    step = pl.program_id(0)
    ctx = gathered(mirror_ref, ctx_ref)
    lines, _, rows, _ = w_ref.shape
    for part in range(lines):
        total_ref[step * lines + part] = first_ref[part] + jnp.dot(
            w_ref[part, 0], ctx, preferred_element_type=jnp.float32
        )

    @pl.when(step == pl.num_programs(0) - 1)
    def _():
        pieces = []
        for outer in range(rows // cols):
            for y in range(total_ref.shape[0]):
                pieces.append(total_ref[y, outer * cols : (outer + 1) * cols, :])
        out_ref[...] = jnp.concatenate(pieces, axis=0).astype(jnp.bfloat16)


def project(head, mirror, w, ctx, cols, first=None):
    count, _, rows, depth = w.shape
    tok = ctx.shape[2]
    step = PROJECT_STEP
    totals = pl.BlockSpec((step, rows, tok), lambda i: (i, 0, 0))
    in_specs = [
        pl.BlockSpec(memory_space=pltpu.SMEM),
        pl.BlockSpec((step, 1, rows, depth), lambda i: (i, head, 0, 0)),
        pl.BlockSpec(ctx.shape, lambda i: (0, 0, 0)),
    ]
    options = dict(
        grid=(count // step,),
        compiler_params=pltpu.CompilerParams(vmem_limit_bytes=PROJECT_VMEM),
        cost_estimate=pl.CostEstimate(
            flops=2 * count * rows * depth * tok, bytes_accessed=2 * count * rows * depth, transcendentals=0
        ),
    )
    if first is None:
        return pl.pallas_call(
            project_first_kernel,
            in_specs=in_specs,
            out_specs=totals,
            out_shape=jax.ShapeDtypeStruct((count, rows, tok), jnp.float32),
            name="project_first",
            **options,
        )(mirror, w, ctx)
    return pl.pallas_call(
        functools.partial(project_last_kernel, cols),
        in_specs=in_specs + [totals],
        out_specs=pl.BlockSpec((count * rows, tok), lambda i: (0, 0)),
        out_shape=jax.ShapeDtypeStruct((count * rows, tok), jnp.bfloat16),
        scratch_shapes=[pltpu.VMEM((count, rows, tok), jnp.float32)],
        name="project_last",
        **options,
    )(mirror, w, ctx, first)


def columns(mirror_ref, chunk, width):
    return pl.ds(pl.multiple_of((chunk ^ mirror_ref[0]) * width, width), width)


def pack_kernel(mirror_ref, k_ref, w_ref, out_ref):
    groups, _, width = out_ref.shape
    tok = k_ref.shape[0]
    half = width // 2
    cols = w_ref.shape[0]
    for g in range(groups):
        out_ref[g, :tok, :] = k_ref[:, columns(mirror_ref, g, width)]
        part = w_ref[:, (g % 2) * half : (g % 2 + 1) * half]
        out_ref[g, tok:, :half] = part[:EXTRA]
        out_ref[g, tok:, half:] = jnp.concatenate(
            [part[EXTRA:], jnp.zeros((2 * EXTRA - cols, half), part.dtype)], axis=0
        )


def pack(mirror, k, wt):
    tok, width = k.shape[0], wt.shape[1]
    return pl.pallas_call(
        pack_kernel,
        in_specs=[pl.BlockSpec(memory_space=pltpu.SMEM)] + [pl.BlockSpec(memory_space=pltpu.VMEM)] * 2,
        out_shape=jax.ShapeDtypeStruct((8, tok + EXTRA, width), k.dtype),
        compiler_params=pltpu.CompilerParams(vmem_limit_bytes=VMEM),
        name="pack",
    )(mirror, k, wt)


def join_kernel(mirror_ref, v_ref, q_ref, out_ref):
    groups, rows, width = out_ref.shape
    tok = rows // 2
    for g in range(groups):
        out_ref[g, :tok, :] = v_ref[:, columns(mirror_ref, g, width)]
        out_ref[g, tok:, :] = q_ref[:, columns(mirror_ref, g, width)]


def join_heads(mirror, v, q):
    tok, width = v.shape
    return pl.pallas_call(
        join_kernel,
        in_specs=[pl.BlockSpec(memory_space=pltpu.SMEM)] + [pl.BlockSpec(memory_space=pltpu.VMEM)] * 2,
        out_shape=jax.ShapeDtypeStruct((8, 2 * tok, width // 8), v.dtype),
        compiler_params=pltpu.CompilerParams(vmem_limit_bytes=VMEM),
        name="join_heads",
    )(mirror, v, q)


def unpack_kernel(in_ref, k_ref, w_ref):
    groups, tok, width = k_ref.shape
    half = width // 2
    for g in range(groups):
        k_ref[g] = in_ref[g, :tok, :]
        w_ref[:EXTRA, g * half : (g + 1) * half] = in_ref[g, tok:, :half]
        w_ref[EXTRA:, g * half : (g + 1) * half] = in_ref[g, tok:, half:]


def unpack(moved):
    groups, rows, width = moved.shape
    tok = rows - EXTRA
    return pl.pallas_call(
        unpack_kernel,
        out_shape=[
            jax.ShapeDtypeStruct((groups, tok, width), moved.dtype),
            jax.ShapeDtypeStruct((2 * EXTRA, groups * width // 2), moved.dtype),
        ],
        compiler_params=pltpu.CompilerParams(vmem_limit_bytes=VMEM),
        name="unpack",
    )(moved)


def tighten_kernel(cols, in_ref, out_ref):
    rows = 2 * EXTRA
    pieces = []
    for x in range(in_ref.shape[0]):
        for z in range(2):
            pieces.append(in_ref[x, z * rows : z * rows + cols, :].astype(jnp.float32))
    out_ref[...] = jnp.concatenate(pieces, axis=0).astype(out_ref.dtype)


def tighten(line, cols):
    count, _, depth = line.shape
    return pl.pallas_call(
        functools.partial(tighten_kernel, cols),
        out_shape=jax.ShapeDtypeStruct((2 * count * cols, depth), line.dtype),
        compiler_params=pltpu.CompilerParams(vmem_limit_bytes=VMEM),
        name="tighten",
    )(line)


def to_heads(chunks):
    return lax.all_to_all(chunks, HEAD, split_axis=0, concat_axis=0)


def behind_kernel(ok_ref, kp_ref, kn_ref, out_ref):
    for side in range(2):
        out_ref[side] = ok_ref[side]


def behind(ok, kp, kn, hint):
    return pl.pallas_call(
        behind_kernel,
        in_specs=[pl.BlockSpec(memory_space=pltpu.SMEM)] + [pl.BlockSpec(memory_space=pl.ANY)] * 2,
        out_specs=pl.BlockSpec(memory_space=pltpu.SMEM),
        out_shape=jax.ShapeDtypeStruct(ok.shape, ok.dtype),
        cost_estimate=pl.CostEstimate(flops=hint, bytes_accessed=0, transcendentals=0),
        name="behind",
    )(ok, kp, kn)


def to_block(value, step):
    pairs = []
    for b in range(N_BLK):
        to = b + step
        if 0 <= to < N_BLK:
            turn = 6 if (b // 8) % 2 != (to // 8) % 2 else 0
            pairs += [(b * 8 + i, to * 8 + (i ^ turn)) for i in range(8)]
    return lax.ppermute(value, AXES, pairs)


def local(queries, keys, values, w_out):
    tok = queries.shape[0]
    cols, depth = w_out.shape[1], 4 * w_out.shape[0]
    here = lax.axis_index(BLK)
    ok = jnp.stack([here > 0, here < N_BLK - 1]).astype(jnp.int32)
    first = lax.axis_index("zh") == 0
    mirror = jnp.where(first, 0, 6).astype(jnp.int32)[None]
    k, w_rows = unpack(to_heads(pack(mirror, keys, w_out.T)))
    k = k.reshape(8 * tok, -1)

    kp, kn = to_block(k, 1), to_block(k, -1)
    values, k = lax.optimization_barrier((values, k))
    vq = to_heads(join_heads(mirror, values, queries))
    other = lax.ppermute(w_rows, "zh", [(0, 1), (1, 0)])
    pair = jnp.concatenate([jnp.where(first, w_rows, other), jnp.where(first, other, w_rows)])
    line = tighten(lax.all_gather(pair, "x"), cols)
    ok = behind(ok, kp, kn, HINT)
    ok, vq, line = lax.optimization_barrier((ok, vq, line))

    v = [vq[:, :tok, h * HDIM : (h + 1) * HDIM].reshape(8 * tok, HDIM) for h in range(2)]
    vp0, vn0 = to_block(v[0], 1), to_block(v[0], -1)
    vp1, vn1 = to_block(v[1], 1), to_block(v[1], -1)
    weight = lax.all_gather(line, ("y", "c")).reshape(8, 2, 8 * cols, depth)
    acc, total, pp, pn = score(ok, vq, k, kp, kn)
    vp0, vn0, acc = lax.optimization_barrier((vp0, vn0, acc))
    ctx0 = mix(0, ok, pp, pn, vp0, vn0, acc, total, tok)
    ctx0 = to_heads(ctx0)
    ok = behind(ok, vp1, vn1, HINT_LAST)
    ctx1 = to_heads(mix(1, ok, pp, pn, vp1, vn1, acc, total, tok))
    totals = project(0, mirror, weight, ctx0, cols)
    return project(1, mirror, weight, ctx1, cols, totals).T


def solution(mesh):
    cut = Mesh(mesh.devices.reshape(SIZES), AXES)
    return jax.shard_map(
        local,
        mesh=cut,
        in_specs=(P(AXES, None), P(AXES, None), P(AXES, None), P(HEAD, BLK)),
        out_specs=P(AXES, None),
        check_vma=False,
    )
```

```python
import functools
import math

import jax
import jax.numpy as jnp
from jax import lax
from jax.experimental import pallas as pl
from jax.experimental.pallas import tpu as pltpu
from jax.sharding import Mesh, PartitionSpec as P

HDIM = 128
LOG2E = 1.4426950408889634
FACTOR = LOG2E / math.sqrt(HDIM)
AXES = ("x", "zh", "y", "zl", "c")
SIZES = (4, 2, 8, 4, 2)
BLK = ("x", "zh", "y")
HEAD = ("zl", "c")
TILE = 1024
MIX_TILE = 1024
CHUNK = 256
PROJECT_STEP = 4
HINT = 28_750_000_000
PROJECT_VMEM = 56 * 1024 * 1024
DIMS_NT = (((1,), (1,)), ((), ()))
DIMS_TN = (((0,), (0,)), ((), ()))
VMEM = 40 * 1024 * 1024
EXTRA = 16
N_BLK = 64


def score_kernel(ok_ref, q_ref, k_ref, v_ref, kp_ref, kn_ref, acc_ref, total_ref, pp_ref, pn_ref):
    far = jnp.float32(1e30)
    chunks, tok, _ = q_ref.shape
    q = q_ref[...].reshape(chunks * tok, HDIM)
    own = v_ref[...].reshape(chunks * tok, HDIM)
    blocks = ((k_ref, None), (kp_ref, ok_ref[0] > 0), (kn_ref, ok_ref[1] > 0))
    scores, m = [], None
    for block, (keys, ok) in enumerate(blocks):
        largest = None
        for start in range(0, keys.shape[0], CHUNK):
            s = lax.dot_general(keys[start : start + CHUNK], q, DIMS_NT, preferred_element_type=jnp.float32)
            scores.append((block, start, s))
            top = jnp.max(s, axis=0, keepdims=True)
            largest = top if largest is None else jnp.maximum(largest, top)
        largest = largest * FACTOR
        if ok is not None:
            largest = jnp.where(ok, largest, -far)
        m = largest if m is None else jnp.maximum(m, largest)
    shifts = [m if ok is None else jnp.where(ok, m, far) for _, ok in blocks]
    total, acc = jnp.zeros_like(m), None
    for block, start, s in scores:
        raised = jnp.exp2(s * FACTOR - shifts[block])
        total += jnp.sum(raised, axis=0, keepdims=True)
        probs = raised.astype(jnp.bfloat16)
        rows = slice(start, start + CHUNK)
        if block == 0:
            part = lax.dot_general(own[rows], probs, DIMS_TN, preferred_element_type=jnp.float32)
            acc = part if acc is None else acc + part
        else:
            (pp_ref if block == 1 else pn_ref)[0, rows] = probs
    acc_ref[0] = acc
    total_ref[0] = jnp.broadcast_to(total, total_ref.shape[1:])


def score(ok, vq, k, kp, kn):
    rows, width = k.shape
    heads = width // HDIM
    joint = (vq.shape[0], vq.shape[1] // 2, HDIM)
    side = pl.BlockSpec((rows, HDIM), lambda h: (0, h))
    probs = pl.BlockSpec((1, rows, rows), lambda h: (h, 0, 0))
    return pl.pallas_call(
        score_kernel,
        grid=(heads,),
        in_specs=[
            pl.BlockSpec(memory_space=pltpu.SMEM),
            pl.BlockSpec(joint, lambda h: (0, 1, h)),
            side,
            pl.BlockSpec(joint, lambda h: (0, 0, h)),
            side,
            side,
        ],
        out_specs=[
            pl.BlockSpec((1, HDIM, rows), lambda h: (h, 0, 0)),
            pl.BlockSpec((1, 8, rows), lambda h: (h, 0, 0)),
            probs,
            probs,
        ],
        out_shape=[
            jax.ShapeDtypeStruct((heads, HDIM, rows), jnp.float32),
            jax.ShapeDtypeStruct((heads, 8, rows), jnp.float32),
            jax.ShapeDtypeStruct((heads, rows, rows), jnp.bfloat16),
            jax.ShapeDtypeStruct((heads, rows, rows), jnp.bfloat16),
        ],
        compiler_params=pltpu.CompilerParams(vmem_limit_bytes=VMEM),
        cost_estimate=pl.CostEstimate(flops=rows * width, bytes_accessed=rows * width, transcendentals=0),
        name="score",
    )(ok, vq, k, vq, kp, kn)


def mix_kernel(pp_ref, pn_ref, vp_ref, vn_ref, acc_ref, total_ref, out_ref):
    tok = out_ref.shape[2]
    acc = acc_ref[0]
    for probs, values in ((pp_ref, vp_ref), (pn_ref, vn_ref)):
        acc += lax.dot_general(values[...], probs[0], DIMS_TN, preferred_element_type=jnp.float32)
    result = (acc / total_ref[0][:1]).astype(jnp.bfloat16)
    for part in range(out_ref.shape[0]):
        out_ref[part] = result[:, part * tok : (part + 1) * tok]


def mix(pp, pn, vp, vn, acc, total, tok):
    rows, width = vp.shape
    heads = width // HDIM
    tile = min(MIX_TILE, rows)
    side = pl.BlockSpec((rows, HDIM), lambda h, i: (0, h))
    probs = pl.BlockSpec((1, rows, tile), lambda h, i: (h, 0, i))
    return pl.pallas_call(
        mix_kernel,
        grid=(heads, rows // tile),
        in_specs=[
            probs,
            probs,
            side,
            side,
            pl.BlockSpec((1, HDIM, tile), lambda h, i: (h, 0, i)),
            pl.BlockSpec((1, 8, tile), lambda h, i: (h, 0, i)),
        ],
        out_specs=pl.BlockSpec((tile // tok, HDIM, tok), lambda h, i: (i, h, 0)),
        out_shape=jax.ShapeDtypeStruct((rows // tok, width, tok), jnp.bfloat16),
        compiler_params=pltpu.CompilerParams(vmem_limit_bytes=VMEM),
        cost_estimate=pl.CostEstimate(
            flops=4 * rows * rows * width, bytes_accessed=14 * rows * width, transcendentals=0
        ),
        name="mix",
    )(pp, pn, vp, vn, acc, total)


def project_kernel(cols, mirror_ref, w_ref, ctx_ref, out_ref, total_ref):
    step = pl.program_id(0)
    groups, width, _ = ctx_ref.shape
    half = width // 2
    lines, _, rows, _ = w_ref.shape
    ctx = []
    for h in range(2):
        pieces = [ctx_ref[g ^ mirror_ref[0], h * half : (h + 1) * half, :] for g in range(groups)]
        ctx.append(jnp.concatenate(pieces, axis=0))
    for part in range(lines):
        total = jnp.dot(w_ref[part, 0], ctx[0], preferred_element_type=jnp.float32)
        total += jnp.dot(w_ref[part, 1], ctx[1], preferred_element_type=jnp.float32)
        total_ref[step * lines + part] = total

    @pl.when(step == pl.num_programs(0) - 1)
    def _():
        pieces = []
        for outer in range(rows // cols):
            for y in range(total_ref.shape[0]):
                pieces.append(total_ref[y, outer * cols : (outer + 1) * cols, :])
        out_ref[...] = jnp.concatenate(pieces, axis=0).astype(jnp.bfloat16)


def project(mirror, w, ctx, cols):
    count, halves, rows, depth = w.shape
    tok = ctx.shape[2]
    step = PROJECT_STEP
    return pl.pallas_call(
        functools.partial(project_kernel, cols),
        grid=(count // step,),
        in_specs=[
            pl.BlockSpec(memory_space=pltpu.SMEM),
            pl.BlockSpec((step, halves, rows, depth), lambda i: (i, 0, 0, 0)),
            pl.BlockSpec(ctx.shape, lambda i: (0, 0, 0)),
        ],
        out_specs=pl.BlockSpec((count * rows, tok), lambda i: (0, 0)),
        out_shape=jax.ShapeDtypeStruct((count * rows, tok), jnp.bfloat16),
        scratch_shapes=[pltpu.VMEM((count, rows, tok), jnp.float32)],
        compiler_params=pltpu.CompilerParams(vmem_limit_bytes=PROJECT_VMEM),
        cost_estimate=pl.CostEstimate(
            flops=2 * count * rows * depth * halves * tok, bytes_accessed=2 * count * rows * depth * halves, transcendentals=0
        ),
        name="project",
    )(mirror, w, ctx)


def columns(mirror_ref, chunk, width):
    return pl.ds(pl.multiple_of((chunk ^ mirror_ref[0]) * width, width), width)


def pack_kernel(mirror_ref, k_ref, w_ref, out_ref):
    groups, _, width = out_ref.shape
    tok = k_ref.shape[0]
    half = width // 2
    cols = w_ref.shape[0]
    for g in range(groups):
        out_ref[g, :tok, :] = k_ref[:, columns(mirror_ref, g, width)]
        part = w_ref[:, (g % 2) * half : (g % 2 + 1) * half]
        out_ref[g, tok:, :half] = part[:EXTRA]
        out_ref[g, tok:, half:] = jnp.concatenate(
            [part[EXTRA:], jnp.zeros((2 * EXTRA - cols, half), part.dtype)], axis=0
        )


def pack(mirror, k, wt):
    tok, width = k.shape[0], wt.shape[1]
    return pl.pallas_call(
        pack_kernel,
        in_specs=[pl.BlockSpec(memory_space=pltpu.SMEM)] + [pl.BlockSpec(memory_space=pltpu.VMEM)] * 2,
        out_shape=jax.ShapeDtypeStruct((8, tok + EXTRA, width), k.dtype),
        compiler_params=pltpu.CompilerParams(vmem_limit_bytes=VMEM),
        name="pack",
    )(mirror, k, wt)


def join_kernel(mirror_ref, v_ref, q_ref, out_ref):
    groups, rows, width = out_ref.shape
    tok = rows // 2
    for g in range(groups):
        out_ref[g, :tok, :] = v_ref[:, columns(mirror_ref, g, width)]
        out_ref[g, tok:, :] = q_ref[:, columns(mirror_ref, g, width)]


def join_heads(mirror, v, q):
    tok, width = v.shape
    return pl.pallas_call(
        join_kernel,
        in_specs=[pl.BlockSpec(memory_space=pltpu.SMEM)] + [pl.BlockSpec(memory_space=pltpu.VMEM)] * 2,
        out_shape=jax.ShapeDtypeStruct((8, 2 * tok, width // 8), v.dtype),
        compiler_params=pltpu.CompilerParams(vmem_limit_bytes=VMEM),
        name="join_heads",
    )(mirror, v, q)


def unpack_kernel(in_ref, k_ref, w_ref):
    groups, tok, width = k_ref.shape
    half = width // 2
    for g in range(groups):
        k_ref[g] = in_ref[g, :tok, :]
        w_ref[:EXTRA, g * half : (g + 1) * half] = in_ref[g, tok:, :half]
        w_ref[EXTRA:, g * half : (g + 1) * half] = in_ref[g, tok:, half:]


def unpack(moved):
    groups, rows, width = moved.shape
    tok = rows - EXTRA
    return pl.pallas_call(
        unpack_kernel,
        out_shape=[
            jax.ShapeDtypeStruct((groups, tok, width), moved.dtype),
            jax.ShapeDtypeStruct((2 * EXTRA, groups * width // 2), moved.dtype),
        ],
        compiler_params=pltpu.CompilerParams(vmem_limit_bytes=VMEM),
        name="unpack",
    )(moved)


def tighten_kernel(cols, in_ref, out_ref):
    rows = 2 * EXTRA
    pieces = []
    for x in range(in_ref.shape[0]):
        for z in range(2):
            pieces.append(in_ref[x, z * rows : z * rows + cols, :].astype(jnp.float32))
    out_ref[...] = jnp.concatenate(pieces, axis=0).astype(out_ref.dtype)


def tighten(line, cols):
    count, _, depth = line.shape
    return pl.pallas_call(
        functools.partial(tighten_kernel, cols),
        out_shape=jax.ShapeDtypeStruct((2 * count * cols, depth), line.dtype),
        compiler_params=pltpu.CompilerParams(vmem_limit_bytes=VMEM),
        name="tighten",
    )(line)


def to_heads(chunks):
    return lax.all_to_all(chunks, HEAD, split_axis=0, concat_axis=0)


def behind_kernel(ok_ref, kp_ref, kn_ref, out_ref):
    for side in range(2):
        out_ref[side] = ok_ref[side]


def behind(ok, kp, kn):
    return pl.pallas_call(
        behind_kernel,
        in_specs=[pl.BlockSpec(memory_space=pltpu.SMEM)] + [pl.BlockSpec(memory_space=pl.ANY)] * 2,
        out_specs=pl.BlockSpec(memory_space=pltpu.SMEM),
        out_shape=jax.ShapeDtypeStruct(ok.shape, ok.dtype),
        cost_estimate=pl.CostEstimate(flops=HINT, bytes_accessed=0, transcendentals=0),
        name="behind",
    )(ok, kp, kn)


def to_block(value, step):
    pairs = []
    for b in range(N_BLK):
        to = b + step
        if 0 <= to < N_BLK:
            turn = 6 if (b // 8) % 2 != (to // 8) % 2 else 0
            pairs += [(b * 8 + i, to * 8 + (i ^ turn)) for i in range(8)]
    return lax.ppermute(value, AXES, pairs)


def local(queries, keys, values, w_out):
    tok = queries.shape[0]
    cols, depth = w_out.shape[1], 4 * w_out.shape[0]
    here = lax.axis_index(BLK)
    ok = jnp.stack([here > 0, here < N_BLK - 1]).astype(jnp.int32)
    first = lax.axis_index("zh") == 0
    mirror = jnp.where(first, 0, 6).astype(jnp.int32)[None]
    joined = join_heads(mirror, values, queries)
    k, w_rows = unpack(to_heads(pack(mirror, keys, w_out.T)))
    k = k.reshape(8 * tok, -1)

    kp, kn = to_block(k, 1), to_block(k, -1)
    vq, k = lax.optimization_barrier((joined, k))
    vq = to_heads(vq)
    other = lax.ppermute(w_rows, "zh", [(0, 1), (1, 0)])
    pair = jnp.concatenate([jnp.where(first, w_rows, other), jnp.where(first, other, w_rows)])
    line = tighten(lax.all_gather(pair, "x"), cols)
    ok = behind(ok, kp, kn)
    ok, vq, line = lax.optimization_barrier((ok, vq, line))

    v = vq[:, :tok].reshape(8 * tok, -1)
    vp, vn = to_block(v, 1), to_block(v, -1)
    weight = lax.all_gather(line, ("y", "c")).reshape(8, 2, 8 * cols, depth)
    acc, total, pp, pn = score(ok, vq, k, kp, kn)
    vp, vn, acc = lax.optimization_barrier((vp, vn, acc))
    ctx = mix(pp, pn, vp, vn, acc, total, tok)
    return project(mirror, weight, to_heads(ctx), cols).T


def solution(mesh):
    cut = Mesh(mesh.devices.reshape(SIZES), AXES)
    return jax.shard_map(
        local,
        mesh=cut,
        in_specs=(P(AXES, None), P(AXES, None), P(AXES, None), P(HEAD, BLK)),
        out_specs=P(AXES, None),
        check_vma=False,
    )
```

```python
import functools
import math

import jax
import jax.numpy as jnp
from jax import lax
from jax.experimental import pallas as pl
from jax.experimental.pallas import tpu as pltpu
from jax.sharding import Mesh, PartitionSpec as P

HDIM = 128
LOG2E = 1.4426950408889634
FACTOR = LOG2E / math.sqrt(HDIM)
AXES = ("x", "zh", "y", "zl", "c")
SIZES = (4, 2, 8, 4, 2)
BLK = ("x", "zh", "y")
HEAD = ("zl", "c")
TILE = 1024
MIX_TILE = 1024
CHUNK = 256
PROJECT_STEP = 4
HINT = 28_750_000_000
PROJECT_VMEM = 56 * 1024 * 1024
DIMS_NT = (((1,), (1,)), ((), ()))
DIMS_TN = (((0,), (0,)), ((), ()))
VMEM = 40 * 1024 * 1024
EXTRA = 16
N_BLK = 64


def score_kernel(ok_ref, q_ref, k_ref, v_ref, kp_ref, kn_ref, acc_ref, total_ref, pp_ref, pn_ref):
    far = jnp.float32(1e30)
    chunks, tok, _ = q_ref.shape
    q = q_ref[...].reshape(chunks * tok, HDIM)
    own = v_ref[...].reshape(chunks * tok, HDIM)
    blocks = ((k_ref, None), (kp_ref, ok_ref[0] > 0), (kn_ref, ok_ref[1] > 0))
    scores, m = [], None
    for block, (keys, ok) in enumerate(blocks):
        largest = None
        for start in range(0, keys.shape[0], CHUNK):
            s = lax.dot_general(keys[start : start + CHUNK], q, DIMS_NT, preferred_element_type=jnp.float32)
            scores.append((block, start, s))
            top = jnp.max(s, axis=0, keepdims=True)
            largest = top if largest is None else jnp.maximum(largest, top)
        largest = largest * FACTOR
        if ok is not None:
            largest = jnp.where(ok, largest, -far)
        m = largest if m is None else jnp.maximum(m, largest)
    shifts = [m if ok is None else jnp.where(ok, m, far) for _, ok in blocks]
    total, acc = jnp.zeros_like(m), None
    for block, start, s in scores:
        raised = jnp.exp2(s * FACTOR - shifts[block])
        total += jnp.sum(raised, axis=0, keepdims=True)
        probs = raised.astype(jnp.bfloat16)
        rows = slice(start, start + CHUNK)
        if block == 0:
            part = lax.dot_general(own[rows], probs, DIMS_TN, preferred_element_type=jnp.float32)
            acc = part if acc is None else acc + part
        else:
            (pp_ref if block == 1 else pn_ref)[0, rows] = probs
    acc_ref[0] = acc
    total_ref[0] = jnp.broadcast_to(total, total_ref.shape[1:])


def score(ok, vq, k, kp, kn):
    rows, width = k.shape
    heads = width // HDIM
    joint = (vq.shape[0], vq.shape[1] // 2, HDIM)
    side = pl.BlockSpec((rows, HDIM), lambda h: (0, h))
    probs = pl.BlockSpec((1, rows, rows), lambda h: (h, 0, 0))
    return pl.pallas_call(
        score_kernel,
        grid=(heads,),
        in_specs=[
            pl.BlockSpec(memory_space=pltpu.SMEM),
            pl.BlockSpec(joint, lambda h: (0, 1, h)),
            side,
            pl.BlockSpec(joint, lambda h: (0, 0, h)),
            side,
            side,
        ],
        out_specs=[
            pl.BlockSpec((1, HDIM, rows), lambda h: (h, 0, 0)),
            pl.BlockSpec((1, 8, rows), lambda h: (h, 0, 0)),
            probs,
            probs,
        ],
        out_shape=[
            jax.ShapeDtypeStruct((heads, HDIM, rows), jnp.float32),
            jax.ShapeDtypeStruct((heads, 8, rows), jnp.float32),
            jax.ShapeDtypeStruct((heads, rows, rows), jnp.bfloat16),
            jax.ShapeDtypeStruct((heads, rows, rows), jnp.bfloat16),
        ],
        compiler_params=pltpu.CompilerParams(vmem_limit_bytes=VMEM),
        cost_estimate=pl.CostEstimate(flops=rows * width, bytes_accessed=rows * width, transcendentals=0),
        name="score",
    )(ok, vq, k, vq, kp, kn)


def mix_kernel(pp_ref, pn_ref, vp_ref, vn_ref, acc_ref, total_ref, out_ref):
    tok = out_ref.shape[2]
    acc = acc_ref[0]
    for probs, values in ((pp_ref, vp_ref), (pn_ref, vn_ref)):
        acc += lax.dot_general(values[...], probs[0], DIMS_TN, preferred_element_type=jnp.float32)
    result = (acc / total_ref[0][:1]).astype(jnp.bfloat16)
    for part in range(out_ref.shape[0]):
        out_ref[part] = result[:, part * tok : (part + 1) * tok]


def mix(pp, pn, vp, vn, acc, total, tok):
    rows, width = vp.shape
    heads = width // HDIM
    tile = min(MIX_TILE, rows)
    side = pl.BlockSpec((rows, HDIM), lambda h, i: (0, h))
    probs = pl.BlockSpec((1, rows, tile), lambda h, i: (h, 0, i))
    return pl.pallas_call(
        mix_kernel,
        grid=(heads, rows // tile),
        in_specs=[
            probs,
            probs,
            side,
            side,
            pl.BlockSpec((1, HDIM, tile), lambda h, i: (h, 0, i)),
            pl.BlockSpec((1, 8, tile), lambda h, i: (h, 0, i)),
        ],
        out_specs=pl.BlockSpec((tile // tok, HDIM, tok), lambda h, i: (i, h, 0)),
        out_shape=jax.ShapeDtypeStruct((rows // tok, width, tok), jnp.bfloat16),
        compiler_params=pltpu.CompilerParams(vmem_limit_bytes=VMEM),
        cost_estimate=pl.CostEstimate(
            flops=4 * rows * rows * width, bytes_accessed=14 * rows * width, transcendentals=0
        ),
        name="mix",
    )(pp, pn, vp, vn, acc, total)


def project_kernel(cols, mirror_ref, w_ref, ctx_ref, out_ref, total_ref):
    step = pl.program_id(0)
    groups, width, _ = ctx_ref.shape
    half = width // 2
    lines, _, rows, _ = w_ref.shape
    ctx = []
    for h in range(2):
        pieces = [ctx_ref[g ^ mirror_ref[0], h * half : (h + 1) * half, :] for g in range(groups)]
        ctx.append(jnp.concatenate(pieces, axis=0))
    for part in range(lines):
        total = jnp.dot(w_ref[part, 0], ctx[0], preferred_element_type=jnp.float32)
        total += jnp.dot(w_ref[part, 1], ctx[1], preferred_element_type=jnp.float32)
        total_ref[step * lines + part] = total

    @pl.when(step == pl.num_programs(0) - 1)
    def _():
        pieces = []
        for outer in range(rows // cols):
            for y in range(total_ref.shape[0]):
                pieces.append(total_ref[y, outer * cols : (outer + 1) * cols, :])
        out_ref[...] = jnp.concatenate(pieces, axis=0).astype(jnp.bfloat16)


def project(mirror, w, ctx, cols):
    count, halves, rows, depth = w.shape
    tok = ctx.shape[2]
    step = PROJECT_STEP
    return pl.pallas_call(
        functools.partial(project_kernel, cols),
        grid=(count // step,),
        in_specs=[
            pl.BlockSpec(memory_space=pltpu.SMEM),
            pl.BlockSpec((step, halves, rows, depth), lambda i: (i, 0, 0, 0)),
            pl.BlockSpec(ctx.shape, lambda i: (0, 0, 0)),
        ],
        out_specs=pl.BlockSpec((count * rows, tok), lambda i: (0, 0)),
        out_shape=jax.ShapeDtypeStruct((count * rows, tok), jnp.bfloat16),
        scratch_shapes=[pltpu.VMEM((count, rows, tok), jnp.float32)],
        compiler_params=pltpu.CompilerParams(vmem_limit_bytes=PROJECT_VMEM),
        cost_estimate=pl.CostEstimate(
            flops=2 * count * rows * depth * halves * tok, bytes_accessed=2 * count * rows * depth * halves, transcendentals=0
        ),
        name="project",
    )(mirror, w, ctx)


def columns(mirror_ref, chunk, width):
    return pl.ds(pl.multiple_of((chunk ^ mirror_ref[0]) * width, width), width)


def pack_kernel(mirror_ref, k_ref, w_ref, out_ref, sems):
    groups, _, width = out_ref.shape
    tok = k_ref.shape[0]
    half = width // 2
    cols = w_ref.shape[0]
    copies = []
    for g in range(groups):
        copies.append(
            pltpu.make_async_copy(
                k_ref.at[:, columns(mirror_ref, g, width)], out_ref.at[g, pl.ds(0, tok), :], sems.at[g]
            )
        )
        copies[g].start()
    for g in range(groups):
        part = w_ref[:, (g % 2) * half : (g % 2 + 1) * half]
        out_ref[g, tok:, :half] = part[:EXTRA]
        out_ref[g, tok:, half:] = jnp.concatenate(
            [part[EXTRA:], jnp.zeros((2 * EXTRA - cols, half), part.dtype)], axis=0
        )
    for copy in copies:
        copy.wait()


def pack(mirror, k, wt):
    tok, width = k.shape[0], wt.shape[1]
    return pl.pallas_call(
        pack_kernel,
        in_specs=[
            pl.BlockSpec(memory_space=pltpu.SMEM),
            pl.BlockSpec(memory_space=pltpu.HBM),
            pl.BlockSpec(memory_space=pltpu.VMEM),
        ],
        scratch_shapes=[pltpu.SemaphoreType.DMA((8,))],
        out_shape=jax.ShapeDtypeStruct((8, tok + EXTRA, width), k.dtype),
        compiler_params=pltpu.CompilerParams(vmem_limit_bytes=60 * 1024 * 1024),
        name="pack",
    )(mirror, k, wt)


def join_kernel(mirror_ref, v_ref, q_ref, out_ref):
    groups, rows, width = out_ref.shape
    tok = rows // 2
    for g in range(groups):
        out_ref[g, :tok, :] = v_ref[:, columns(mirror_ref, g, width)]
        out_ref[g, tok:, :] = q_ref[:, columns(mirror_ref, g, width)]


def join_heads(mirror, v, q):
    tok, width = v.shape
    return pl.pallas_call(
        join_kernel,
        in_specs=[pl.BlockSpec(memory_space=pltpu.SMEM)] + [pl.BlockSpec(memory_space=pltpu.VMEM)] * 2,
        out_shape=jax.ShapeDtypeStruct((8, 2 * tok, width // 8), v.dtype),
        compiler_params=pltpu.CompilerParams(vmem_limit_bytes=VMEM),
        name="join_heads",
    )(mirror, v, q)


def unpack_kernel(in_ref, k_ref, w_ref):
    groups, tok, width = k_ref.shape
    half = width // 2
    for g in range(groups):
        k_ref[g] = in_ref[g, :tok, :]
        w_ref[:EXTRA, g * half : (g + 1) * half] = in_ref[g, tok:, :half]
        w_ref[EXTRA:, g * half : (g + 1) * half] = in_ref[g, tok:, half:]


def unpack(moved):
    groups, rows, width = moved.shape
    tok = rows - EXTRA
    return pl.pallas_call(
        unpack_kernel,
        out_shape=[
            jax.ShapeDtypeStruct((groups, tok, width), moved.dtype),
            jax.ShapeDtypeStruct((2 * EXTRA, groups * width // 2), moved.dtype),
        ],
        compiler_params=pltpu.CompilerParams(vmem_limit_bytes=VMEM),
        name="unpack",
    )(moved)


def tighten_kernel(cols, in_ref, out_ref):
    rows = 2 * EXTRA
    pieces = []
    for x in range(in_ref.shape[0]):
        for z in range(2):
            pieces.append(in_ref[x, z * rows : z * rows + cols, :].astype(jnp.float32))
    out_ref[...] = jnp.concatenate(pieces, axis=0).astype(out_ref.dtype)


def tighten(line, cols):
    count, _, depth = line.shape
    return pl.pallas_call(
        functools.partial(tighten_kernel, cols),
        out_shape=jax.ShapeDtypeStruct((2 * count * cols, depth), line.dtype),
        compiler_params=pltpu.CompilerParams(vmem_limit_bytes=VMEM),
        name="tighten",
    )(line)


def to_heads(chunks):
    return lax.all_to_all(chunks, HEAD, split_axis=0, concat_axis=0)


def behind_kernel(ok_ref, kp_ref, kn_ref, out_ref):
    for side in range(2):
        out_ref[side] = ok_ref[side]


def behind(ok, kp, kn):
    return pl.pallas_call(
        behind_kernel,
        in_specs=[pl.BlockSpec(memory_space=pltpu.SMEM)] + [pl.BlockSpec(memory_space=pl.ANY)] * 2,
        out_specs=pl.BlockSpec(memory_space=pltpu.SMEM),
        out_shape=jax.ShapeDtypeStruct(ok.shape, ok.dtype),
        cost_estimate=pl.CostEstimate(flops=HINT, bytes_accessed=0, transcendentals=0),
        name="behind",
    )(ok, kp, kn)


def to_block(value, step):
    pairs = []
    for b in range(N_BLK):
        to = b + step
        if 0 <= to < N_BLK:
            turn = 6 if (b // 8) % 2 != (to // 8) % 2 else 0
            pairs += [(b * 8 + i, to * 8 + (i ^ turn)) for i in range(8)]
    return lax.ppermute(value, AXES, pairs)


def local(queries, keys, values, w_out):
    tok = queries.shape[0]
    cols, depth = w_out.shape[1], 4 * w_out.shape[0]
    here = lax.axis_index(BLK)
    ok = jnp.stack([here > 0, here < N_BLK - 1]).astype(jnp.int32)
    first = lax.axis_index("zh") == 0
    mirror = jnp.where(first, 0, 6).astype(jnp.int32)[None]
    joined = join_heads(mirror, values, queries)
    k, w_rows = unpack(to_heads(pack(mirror, keys, w_out.T)))
    k = k.reshape(8 * tok, -1)

    kp, kn = to_block(k, 1), to_block(k, -1)
    vq, k = lax.optimization_barrier((joined, k))
    vq = to_heads(vq)
    other = lax.ppermute(w_rows, "zh", [(0, 1), (1, 0)])
    pair = jnp.concatenate([jnp.where(first, w_rows, other), jnp.where(first, other, w_rows)])
    line = tighten(lax.all_gather(pair, "x"), cols)
    ok = behind(ok, kp, kn)
    ok, vq, line = lax.optimization_barrier((ok, vq, line))

    v = vq[:, :tok].reshape(8 * tok, -1)
    vp, vn = to_block(v, 1), to_block(v, -1)
    weight = lax.all_gather(line, ("y", "c")).reshape(8, 2, 8 * cols, depth)
    acc, total, pp, pn = score(ok, vq, k, kp, kn)
    vp, vn, acc = lax.optimization_barrier((vp, vn, acc))
    ctx = mix(pp, pn, vp, vn, acc, total, tok)
    return project(mirror, weight, to_heads(ctx), cols).T


def solution(mesh):
    cut = Mesh(mesh.devices.reshape(SIZES), AXES)
    return jax.shard_map(
        local,
        mesh=cut,
        in_specs=(P(AXES, None), P(AXES, None), P(AXES, None), P(HEAD, BLK)),
        out_specs=P(AXES, None),
        check_vma=False,
    )
```

```python
import functools
import math

import jax
import jax.numpy as jnp
from jax import lax
from jax.experimental import pallas as pl
from jax.experimental.pallas import tpu as pltpu
from jax.sharding import Mesh, PartitionSpec as P

HDIM = 128
LOG2E = 1.4426950408889634
FACTOR = LOG2E / math.sqrt(HDIM)
AXES = ("x", "zh", "y", "zl", "c")
SIZES = (4, 2, 8, 4, 2)
BLK = ("x", "zh", "y")
HEAD = ("zl", "c")
TILE = 1024
MIX_TILE = 1024
CHUNK = 256
PROJECT_STEP = 4
HINT = 4_600_000_000
PROJECT_VMEM = 56 * 1024 * 1024
DIMS_NT = (((1,), (1,)), ((), ()))
DIMS_TN = (((0,), (0,)), ((), ()))
VMEM = 40 * 1024 * 1024
EXTRA = 16
N_BLK = 64


def score_kernel(ok_ref, q_ref, k_ref, v_ref, kp_ref, kn_ref, acc_ref, total_ref, pp_ref, pn_ref):
    far = jnp.float32(1e30)
    chunks, tok, _ = q_ref.shape
    q = q_ref[...].reshape(chunks * tok, HDIM)
    own = v_ref[...].reshape(chunks * tok, HDIM)
    blocks = ((k_ref, None), (kp_ref, ok_ref[0] > 0), (kn_ref, ok_ref[1] > 0))
    scores, m = [], None
    for block, (keys, ok) in enumerate(blocks):
        largest = None
        for start in range(0, keys.shape[0], CHUNK):
            s = lax.dot_general(keys[start : start + CHUNK], q, DIMS_NT, preferred_element_type=jnp.float32)
            scores.append((block, start, s))
            top = jnp.max(s, axis=0, keepdims=True)
            largest = top if largest is None else jnp.maximum(largest, top)
        largest = largest * FACTOR
        if ok is not None:
            largest = jnp.where(ok, largest, -far)
        m = largest if m is None else jnp.maximum(m, largest)
    shifts = [m if ok is None else jnp.where(ok, m, far) for _, ok in blocks]
    total, acc = jnp.zeros_like(m), None
    for block, start, s in scores:
        raised = jnp.exp2(s * FACTOR - shifts[block])
        total += jnp.sum(raised, axis=0, keepdims=True)
        probs = raised.astype(jnp.bfloat16)
        rows = slice(start, start + CHUNK)
        if block == 0:
            part = lax.dot_general(own[rows], probs, DIMS_TN, preferred_element_type=jnp.float32)
            acc = part if acc is None else acc + part
        else:
            (pp_ref if block == 1 else pn_ref)[0, rows] = probs
    acc_ref[0] = acc
    total_ref[0] = jnp.broadcast_to(total, total_ref.shape[1:])


def score(ok, vq, k, kp, kn):
    rows, width = k.shape
    heads = width // HDIM
    joint = (vq.shape[0], vq.shape[1] // 2, HDIM)
    side = pl.BlockSpec((rows, HDIM), lambda h: (0, h))
    probs = pl.BlockSpec((1, rows, rows), lambda h: (h, 0, 0))
    return pl.pallas_call(
        score_kernel,
        grid=(heads,),
        in_specs=[
            pl.BlockSpec(memory_space=pltpu.SMEM),
            pl.BlockSpec(joint, lambda h: (0, 1, h)),
            side,
            pl.BlockSpec(joint, lambda h: (0, 0, h)),
            side,
            side,
        ],
        out_specs=[
            pl.BlockSpec((1, HDIM, rows), lambda h: (h, 0, 0)),
            pl.BlockSpec((1, 8, rows), lambda h: (h, 0, 0)),
            probs,
            probs,
        ],
        out_shape=[
            jax.ShapeDtypeStruct((heads, HDIM, rows), jnp.float32),
            jax.ShapeDtypeStruct((heads, 8, rows), jnp.float32),
            jax.ShapeDtypeStruct((heads, rows, rows), jnp.bfloat16),
            jax.ShapeDtypeStruct((heads, rows, rows), jnp.bfloat16),
        ],
        compiler_params=pltpu.CompilerParams(vmem_limit_bytes=VMEM),
        cost_estimate=pl.CostEstimate(flops=rows * width, bytes_accessed=rows * width, transcendentals=0),
        name="score",
    )(ok, vq, k, vq, kp, kn)


def mix_kernel(pp_ref, pn_ref, vp_ref, vn_ref, acc_ref, total_ref, out_ref):
    tok = out_ref.shape[2]
    acc = acc_ref[0]
    for probs, values in ((pp_ref, vp_ref), (pn_ref, vn_ref)):
        acc += lax.dot_general(values[...], probs[0], DIMS_TN, preferred_element_type=jnp.float32)
    result = (acc / total_ref[0][:1]).astype(jnp.bfloat16)
    for part in range(out_ref.shape[0]):
        out_ref[part] = result[:, part * tok : (part + 1) * tok]


def mix(pp, pn, vp, vn, acc, total, tok):
    rows, width = vp.shape
    heads = width // HDIM
    tile = min(MIX_TILE, rows)
    side = pl.BlockSpec((rows, HDIM), lambda h, i: (0, h))
    probs = pl.BlockSpec((1, rows, tile), lambda h, i: (h, 0, i))
    return pl.pallas_call(
        mix_kernel,
        grid=(heads, rows // tile),
        in_specs=[
            probs,
            probs,
            side,
            side,
            pl.BlockSpec((1, HDIM, tile), lambda h, i: (h, 0, i)),
            pl.BlockSpec((1, 8, tile), lambda h, i: (h, 0, i)),
        ],
        out_specs=pl.BlockSpec((tile // tok, HDIM, tok), lambda h, i: (i, h, 0)),
        out_shape=jax.ShapeDtypeStruct((rows // tok, width, tok), jnp.bfloat16),
        compiler_params=pltpu.CompilerParams(vmem_limit_bytes=VMEM),
        cost_estimate=pl.CostEstimate(
            flops=4 * rows * rows * width, bytes_accessed=14 * rows * width, transcendentals=0
        ),
        name="mix",
    )(pp, pn, vp, vn, acc, total)


def project_kernel(cols, mirror_ref, w_ref, ctx_ref, out_ref, total_ref):
    step = pl.program_id(0)
    groups, width, _ = ctx_ref.shape
    half = width // 2
    lines, _, rows, _ = w_ref.shape
    ctx = []
    for h in range(2):
        pieces = [ctx_ref[g ^ mirror_ref[0], h * half : (h + 1) * half, :] for g in range(groups)]
        ctx.append(jnp.concatenate(pieces, axis=0))
    for part in range(lines):
        total = jnp.dot(w_ref[part, 0], ctx[0], preferred_element_type=jnp.float32)
        total += jnp.dot(w_ref[part, 1], ctx[1], preferred_element_type=jnp.float32)
        total_ref[step * lines + part] = total

    @pl.when(step == pl.num_programs(0) - 1)
    def _():
        pieces = []
        for outer in range(rows // cols):
            for y in range(total_ref.shape[0]):
                pieces.append(total_ref[y, outer * cols : (outer + 1) * cols, :])
        out_ref[...] = jnp.concatenate(pieces, axis=0).astype(jnp.bfloat16)


def project(mirror, w, ctx, cols):
    count, halves, rows, depth = w.shape
    tok = ctx.shape[2]
    step = PROJECT_STEP
    return pl.pallas_call(
        functools.partial(project_kernel, cols),
        grid=(count // step,),
        in_specs=[
            pl.BlockSpec(memory_space=pltpu.SMEM),
            pl.BlockSpec((step, halves, rows, depth), lambda i: (i, 0, 0, 0)),
            pl.BlockSpec(ctx.shape, lambda i: (0, 0, 0)),
        ],
        out_specs=pl.BlockSpec((count * rows, tok), lambda i: (0, 0)),
        out_shape=jax.ShapeDtypeStruct((count * rows, tok), jnp.bfloat16),
        scratch_shapes=[pltpu.VMEM((count, rows, tok), jnp.float32)],
        compiler_params=pltpu.CompilerParams(vmem_limit_bytes=PROJECT_VMEM),
        cost_estimate=pl.CostEstimate(
            flops=2 * count * rows * depth * halves * tok, bytes_accessed=2 * count * rows * depth * halves, transcendentals=0
        ),
        name="project",
    )(mirror, w, ctx)


def columns(mirror_ref, chunk, width):
    return pl.ds(pl.multiple_of((chunk ^ mirror_ref[0]) * width, width), width)


def pack_kernel(mirror_ref, k_ref, w_ref, out_ref):
    groups, _, width = out_ref.shape
    tok = k_ref.shape[0]
    half = width // 2
    cols = w_ref.shape[0]
    for g in range(groups):
        out_ref[g, :tok, :] = k_ref[:, columns(mirror_ref, g, width)]
        part = w_ref[:, (g % 2) * half : (g % 2 + 1) * half]
        out_ref[g, tok:, :half] = part[:EXTRA]
        out_ref[g, tok:, half:] = jnp.concatenate(
            [part[EXTRA:], jnp.zeros((2 * EXTRA - cols, half), part.dtype)], axis=0
        )


def pack(mirror, k, wt):
    tok, width = k.shape[0], wt.shape[1]
    return pl.pallas_call(
        pack_kernel,
        in_specs=[pl.BlockSpec(memory_space=pltpu.SMEM)] + [pl.BlockSpec(memory_space=pltpu.VMEM)] * 2,
        out_shape=jax.ShapeDtypeStruct((8, tok + EXTRA, width), k.dtype),
        compiler_params=pltpu.CompilerParams(vmem_limit_bytes=VMEM),
        name="pack",
    )(mirror, k, wt)


def join_kernel(mirror_ref, v_ref, q_ref, out_ref):
    groups, rows, width = out_ref.shape
    tok = rows // 2
    for g in range(groups):
        out_ref[g, :tok, :] = v_ref[:, columns(mirror_ref, g, width)]
        out_ref[g, tok:, :] = q_ref[:, columns(mirror_ref, g, width)]


def join_heads(mirror, v, q):
    tok, width = v.shape
    return pl.pallas_call(
        join_kernel,
        in_specs=[pl.BlockSpec(memory_space=pltpu.SMEM)] + [pl.BlockSpec(memory_space=pltpu.VMEM)] * 2,
        out_shape=jax.ShapeDtypeStruct((8, 2 * tok, width // 8), v.dtype),
        compiler_params=pltpu.CompilerParams(vmem_limit_bytes=VMEM),
        name="join_heads",
    )(mirror, v, q)


def unpack_kernel(in_ref, k_ref, w_ref):
    groups, tok, width = k_ref.shape
    half = width // 2
    for g in range(groups):
        k_ref[g] = in_ref[g, :tok, :]
        w_ref[:EXTRA, g * half : (g + 1) * half] = in_ref[g, tok:, :half]
        w_ref[EXTRA:, g * half : (g + 1) * half] = in_ref[g, tok:, half:]


def unpack(moved):
    groups, rows, width = moved.shape
    tok = rows - EXTRA
    return pl.pallas_call(
        unpack_kernel,
        out_shape=[
            jax.ShapeDtypeStruct((groups, tok, width), moved.dtype),
            jax.ShapeDtypeStruct((2 * EXTRA, groups * width // 2), moved.dtype),
        ],
        compiler_params=pltpu.CompilerParams(vmem_limit_bytes=VMEM),
        name="unpack",
    )(moved)


def tighten_kernel(cols, in_ref, out_ref):
    rows = 2 * EXTRA
    pieces = []
    for x in range(in_ref.shape[0]):
        for z in range(2):
            pieces.append(in_ref[x, z * rows : z * rows + cols, :].astype(jnp.float32))
    out_ref[...] = jnp.concatenate(pieces, axis=0).astype(out_ref.dtype)


def tighten(line, cols):
    count, _, depth = line.shape
    return pl.pallas_call(
        functools.partial(tighten_kernel, cols),
        out_shape=jax.ShapeDtypeStruct((2 * count * cols, depth), line.dtype),
        compiler_params=pltpu.CompilerParams(vmem_limit_bytes=VMEM),
        name="tighten",
    )(line)


def to_heads(chunks):
    return lax.all_to_all(chunks, HEAD, split_axis=0, concat_axis=0)


def behind_kernel(ok_ref, kp_ref, kn_ref, out_ref):
    for side in range(2):
        out_ref[side] = ok_ref[side]


def behind(ok, kp, kn):
    return pl.pallas_call(
        behind_kernel,
        in_specs=[pl.BlockSpec(memory_space=pltpu.SMEM)] + [pl.BlockSpec(memory_space=pl.ANY)] * 2,
        out_specs=pl.BlockSpec(memory_space=pltpu.SMEM),
        out_shape=jax.ShapeDtypeStruct(ok.shape, ok.dtype),
        cost_estimate=pl.CostEstimate(flops=HINT, bytes_accessed=0, transcendentals=0),
        name="behind",
    )(ok, kp, kn)


def to_block(value, step):
    pairs = []
    for b in range(N_BLK):
        to = b + step
        if 0 <= to < N_BLK:
            turn = 6 if (b // 8) % 2 != (to // 8) % 2 else 0
            pairs += [(b * 8 + i, to * 8 + (i ^ turn)) for i in range(8)]
    return lax.ppermute(value, AXES, pairs)


def local(queries, keys, values, w_out):
    tok = queries.shape[0]
    cols, depth = w_out.shape[1], 4 * w_out.shape[0]
    here = lax.axis_index(BLK)
    ok = jnp.stack([here > 0, here < N_BLK - 1]).astype(jnp.int32)
    first = lax.axis_index("zh") == 0
    mirror = jnp.where(first, 0, 6).astype(jnp.int32)[None]
    joined = join_heads(mirror, values, queries)
    k, w_rows = unpack(to_heads(pack(mirror, keys, w_out.T)))
    k = k.reshape(8 * tok, -1)

    kp, kn = to_block(k, 1), to_block(k, -1)
    other = lax.ppermute(w_rows, "zh", [(0, 1), (1, 0)])
    vq, other = lax.optimization_barrier((joined, other))
    vq = to_heads(vq)
    pair = jnp.concatenate([jnp.where(first, w_rows, other), jnp.where(first, other, w_rows)])
    line = tighten(lax.all_gather(pair, "x"), cols)
    ok = behind(ok, kp, kn)
    ok, vq, line = lax.optimization_barrier((ok, vq, line))

    v = vq[:, :tok].reshape(8 * tok, -1)
    vp, vn = to_block(v, 1), to_block(v, -1)
    weight = lax.all_gather(line, ("y", "c")).reshape(8, 2, 8 * cols, depth)
    acc, total, pp, pn = score(ok, vq, k, kp, kn)
    vp, vn, acc = lax.optimization_barrier((vp, vn, acc))
    ctx = mix(pp, pn, vp, vn, acc, total, tok)
    return project(mirror, weight, to_heads(ctx), cols).T


def solution(mesh):
    cut = Mesh(mesh.devices.reshape(SIZES), AXES)
    return jax.shard_map(
        local,
        mesh=cut,
        in_specs=(P(AXES, None), P(AXES, None), P(AXES, None), P(HEAD, BLK)),
        out_specs=P(AXES, None),
        check_vma=False,
    )
```
